256 devices in a mesh: row: 8 (over x_hi, y), col: 8 (over z), fsdp: 4 (over x_lo, core).
Axes of the slice: x: 4 (x_hi: 2, x_lo: 2; x = x_hi * 2 + x_lo), y: 4, z: 8, core: 2. Of those that a mesh axis runs over, the one named last changes fastest.
Arguments:
- tokens: bfloat16 [4, 64, 128, 6144], P('fsdp', 'row', 'col'), may hold values from -6 to 6
- ln_gain: float32 [6144], replicated, may hold values from 0.5 to 1.5
- qkv_blocks: bfloat16 [72, 6, 128, 128], P('fsdp'), may hold values from -0.21875 to 0.21875
- qkv_index: int32 [72, 6], replicated, may hold values from 0 to 47, as said below
- out_blocks: bfloat16 [48, 3, 128, 128], P('fsdp'), may hold values from -0.3125 to 0.3125
- out_index: int32 [48, 3], replicated, may hold values from 0 to 23, as said below
- rel_bias: float32 [24, 81], replicated, may hold values from -2 to 2
Outputs:
- mixed: bfloat16 [4, 64, 128, 6144], P('fsdp', 'row', 'col')
The draws below stay inside these ranges and needn't reach their ends.
Inputs may be any that keep to these rules, and one draw needn't show every extreme that they name: `qkv_index`: each row names 6 different row blocks in increasing order. `out_index`: each row names 3 different row blocks in increasing order.
All inputs are finite; a program needn't handle non-finite values.
Results may differ from the reference program's by a relative error of at most 0.0039.
Values may be sent and summed in bfloat16 or wider, within the bound.
A program may use at most 128 MiB of HBM per device.

```python
import jax
import jax.numpy as jnp
from jax import lax

D = 6144
HD = 128
HEADS = 24
KEEP = 6
KEEP_O = 3
RADIUS = 4
GH = 64
GW = 128
IMAGES = 4


def pick_blocks(key, columns, choice_count, keep_count):
    ranking = jax.random.randint(key, (columns, choice_count), 0, 1 << 20) * choice_count
    ranking = ranking + jnp.arange(choice_count, dtype=jnp.int32)[None, :]
    ranking = ranking.at[0, 0].set(-2).at[0, choice_count - 1].set(-1)
    chosen = jnp.argsort(ranking, axis=1)[:, :keep_count]
    return jnp.sort(chosen, axis=1).astype(jnp.int32)


def draw_qkv_index(key, part):
    key = jax.random.fold_in(key, 11)
    return pick_blocks(key, 3 * HEADS, D // HD, KEEP)


def draw_out_index(key, part):
    key = jax.random.fold_in(key, 23)
    return pick_blocks(key, D // HD, HEADS, KEEP_O)


def block_levels(own_key, extent, cuts, smallest, top_value):
    def one(dim, blocks):
        heights = jax.random.uniform(jax.random.fold_in(jax.random.fold_in(own_key, 6), dim), (blocks,), jnp.float32, smallest / len(cuts), top_value / len(cuts))
        return jnp.repeat(jnp.exp(heights), extent[dim] // blocks).reshape((-1,) + (1,) * (len(extent) - dim - 1))

    gain = one(*cuts[0])
    for cut in cuts[1:]:
        gain = gain * one(*cut)
    return gain


def normal_values(own_key, extent, scale, most, shards=(), held_as=jnp.bfloat16):
    gain = block_levels(own_key, extent, shards, -0.22, 0.18) if shards else 1.0
    values = jax.random.normal(own_key, extent, jnp.float32) * scale * gain
    return jnp.minimum(jnp.maximum(values, -most), most).astype(held_as)


def setup_inputs(seed: int = 0) -> dict:
    streams_of = jax.random.split(jax.random.key(seed), 8)
    tokens = normal_values(streams_of[0], (IMAGES, GH, GW, D), 1.0, 6.0, ((0, 4), (1, 8), (2, 8)))
    ln_gain = jnp.clip(1.0 + 0.1 * jax.random.normal(streams_of[1], (D,), jnp.float32), 0.5, 1.5)
    qkv_blocks = normal_values(streams_of[2], (3 * HEADS, KEEP, HD, HD), (KEEP * HD) ** -0.5, 0.21875, ((0, 4),))
    qkv_index = draw_qkv_index(jax.random.fold_in(streams_of[7], 71), 0)
    out_blocks = normal_values(streams_of[4], (D // HD, KEEP_O, HD, HD), (KEEP_O * HD) ** -0.5, 0.3125, ((0, 4),))
    out_index = draw_out_index(jax.random.fold_in(streams_of[7], 71), 0)
    rel_bias = jnp.clip(jax.random.uniform(streams_of[6], (HEADS, (2 * RADIUS + 1) * (2 * RADIUS + 1)), jnp.float32, -2.0, 2.0), -2.0, 2.0)
    return dict(tokens=tokens, ln_gain=ln_gain, qkv_blocks=qkv_blocks, qkv_index=qkv_index, out_blocks=out_blocks, out_index=out_index, rel_bias=rel_bias)


def block_product(rows_in, blocks, index):
    count = rows_in.shape[0]
    head_size = blocks.shape[2]
    blocks_of = rows_in.reshape(count, -1, head_size)

    def column(args):
        block_set, block_ids = args
        picked = jnp.take(blocks_of, block_ids, axis=1).reshape(count, -1).astype(jnp.float32)
        return jnp.dot(picked, block_set.reshape(-1, head_size).astype(jnp.float32), precision=lax.Precision.HIGHEST)
    result = lax.map(column, (blocks, index))
    return jnp.transpose(result, (1, 0, 2)).reshape(count, -1)

def neighbourhood(query, kv_rim, bias, row_first, col_first, height, width):
    tile_rows, tile_cols, channels = query.shape
    head_count = bias.shape[0]
    head_size = channels // head_count
    window = 2 * RADIUS + 1
    score_scale = 1.0 / jnp.sqrt(jnp.float32(head_size))
    query_wide = query.astype(jnp.float32).reshape(tile_rows, tile_cols, head_count, head_size)
    row_pos = row_first + jnp.arange(tile_rows, dtype=jnp.int32)[:, None]
    col_pos = col_first + jnp.arange(tile_cols, dtype=jnp.int32)[None, :]

    def score(offset):
        offset = offset.astype(jnp.int32)
        offset_row = (offset // window).astype(jnp.int32)
        offset_col = (offset % window).astype(jnp.int32)
        key_tile = lax.dynamic_slice(kv_rim, (offset_row, offset_col, jnp.int32(0)), (tile_rows, tile_cols, channels))
        key_tile = key_tile.astype(jnp.float32).reshape(tile_rows, tile_cols, head_count, head_size)
        logits = lax.optimization_barrier(jnp.sum(query_wide * key_tile, axis=-1)) * score_scale + bias[:, offset]
        key_row = row_pos + offset_row - RADIUS
        key_col = col_pos + offset_col - RADIUS
        inside = (key_row >= 0) & (key_row < height) & (key_col >= 0) & (key_col < width)
        return jnp.where(inside[..., None], jnp.exp(logits), jnp.float32(0.0))
    weights = lax.map(score, jnp.arange(window * window, dtype=jnp.int32))
    denominator = lax.optimization_barrier(jnp.sum(weights, axis=0))
    prob_low = (weights / denominator).astype(jnp.bfloat16)

    def accumulate(offset, running):
        offset = jnp.asarray(offset).astype(jnp.int32)
        offset_row = (offset // window).astype(jnp.int32)
        offset_col = (offset % window).astype(jnp.int32)
        value_tile = lax.dynamic_slice(kv_rim, (offset_row, offset_col, jnp.int32(channels)), (tile_rows, tile_cols, channels))
        value_tile = value_tile.astype(jnp.float32).reshape(tile_rows, tile_cols, head_count, head_size)
        return running + prob_low[offset][..., None].astype(jnp.float32) * value_tile
    start_sum = jnp.zeros((tile_rows, tile_cols, head_count, head_size), jnp.float32)
    running = lax.fori_loop(0, window * window, accumulate, start_sum)
    return running.reshape(tile_rows, tile_cols, channels).astype(jnp.bfloat16)

def reference(tokens, ln_gain, qkv_blocks, qkv_index, out_blocks, out_index, rel_bias):
    count = IMAGES * GH * GW
    widened = tokens.astype(jnp.float32).reshape(count, D)
    average = lax.optimization_barrier(jnp.mean(widened, axis=-1, keepdims=True))
    variance = lax.optimization_barrier(jnp.mean((widened - average) ** 2, axis=-1, keepdims=True))
    normed = ((widened - average) * lax.rsqrt(variance + 1e-06) * ln_gain).astype(jnp.bfloat16)
    projected = block_product(normed, qkv_blocks, qkv_index).astype(jnp.bfloat16)
    projected = projected.reshape(IMAGES, GH, GW, 3 * HEADS * HD)
    channels = HEADS * HD

    def one_slide(slide):
        query = slide[:, :, :channels]
        kv_both = slide[:, :, channels:]
        kv_rim = jnp.pad(kv_both, ((RADIUS, RADIUS), (RADIUS, RADIUS), (0, 0)))
        return neighbourhood(query, kv_rim, rel_bias, jnp.int32(0), jnp.int32(0), GH, GW)
    attended = lax.map(one_slide, projected).reshape(count, channels)
    branch = block_product(attended, out_blocks, out_index)
    mixed = widened + branch
    return mixed.reshape(IMAGES, GH, GW, D).astype(jnp.bfloat16)
```

```python
import functools

import jax
import jax.numpy as jnp
from jax import lax
from jax.experimental import pallas as pl
from jax.experimental.pallas import tpu as pltpu
from jax.sharding import PartitionSpec as P

MESH = pl.DeviceIdType.MESH
HD = 128
HEADS = 24
KEEP = 6
KEEP_O = 3
RADIUS = 4
TH, TW = 8, 16
OWN = TH * TW
ALL = (TH + 2 * RADIUS) * (TW + 2 * RADIUS)
GROUPS = 48
SHARD = 18
SHARD_O = 12
NEG = -1e30
SLOT = dict(S=(128, 64), N=(192, 64), NW=(256, 16), W=(272, 32), SW=(304, 16), NE=(320, 16), E=(336, 32), SE=(368, 16))
SIDES = dict(S=(1, 0), N=(-1, 0), NW=(-1, -1), W=(0, -1), SW=(1, -1), NE=(-1, 1), E=(0, 1), SE=(1, 1))
OPPOSITE = dict(S="N", N="S", NW="SE", SE="NW", NE="SW", SW="NE", W="E", E="W")
NAMES = tuple(SLOT)
X_CB = 12
Z_CB = 6


def kernel(
    qi, oi, tok, left, right, gain, base, wq, wo, out,
    T, N, W, WO, QKV, ATT, B,
    loc, hs, hr, xs, xr, zs, zr, ss, sr, bxs, bxr, bys, byr, bss, bsr,
):
    row, col, fs_ = lax.axis_index("row"), lax.axis_index("col"), lax.axis_index("fsdp")
    x, y, z, k = (row // 4) * 2 + fs_ // 2, row % 4, col, fs_ % 2

    def dev(dx, dy, dz, dk):
        xx, yy, zz, kk = (x + dx) % 4, (y + dy) % 4, (z + dz) % 8, (k + dk) % 2
        return ((xx // 2) * 4 + yy, zz, (xx % 2) * 2 + kk)

    def tile(dr, dc):
        return ((row + dr + 8) % 8, (col + dc + 8) % 8, fs_)

    f_own = fs_
    f_sib = (x % 2) * 2 + (1 - k)
    f_oth = (1 - x % 2) * 2 + k
    f_osb = (1 - x % 2) * 2 + (1 - k)
    cz, cy = z % 2, y % 2
    sib = dev(0, 0, 0, 1)
    xp, xm = dev(1, 0, 0, 0), dev(3, 0, 0, 0)
    yp, ym = dev(0, 1, 0, 0), dev(0, 3, 0, 0)
    zp, zm = dev(0, 0, 1, 0), dev(0, 0, 7, 0)

    def acb(i, color):
        return i + color * (SHARD - 1 - 2 * i)

    c_tok = pltpu.make_async_copy(tok, T.at[pl.ds(0, OWN)], loc.at[0])
    c_wq = pltpu.make_async_copy(wq, W.at[pl.ds(f_own * 108, 108)], loc.at[1])
    c_wo = pltpu.make_async_copy(wo, WO.at[pl.ds(f_own * 36, 36)], loc.at[2])
    c_tok.start()
    c_wq.start()
    c_wo.start()

    partners = [sib, xp, xm, yp, ym, zp, zm, tile(1, 0), tile(-1, 0), tile(1, 1), tile(1, -1), tile(-1, 1), tile(-1, -1)]
    barrier = pltpu.get_barrier_semaphore()
    for p in partners:
        pl.semaphore_signal(barrier, inc=1, device_id=p, device_id_type=MESH)
    pl.semaphore_wait(barrier, len(partners))

    def rc(src, dst, s, r, to):
        return pltpu.make_async_remote_copy(src_ref=src, dst_ref=dst, send_sem=s, recv_sem=r, device_id=to, device_id_type=MESH)

    def cols(f, cb):
        return W.at[pl.ds((f * SHARD + cb) * KEEP, KEEP)]

    def x_send(i):
        cb = acb(i, cz)
        return rc(wq.at[pl.ds(cb * KEEP, KEEP)], cols(f_own, cb), xs.at[i], xr.at[i], xp if (i // 3) % 2 == 0 else xm)

    def x_recv(i):
        d = cols(f_oth, acb(i, cz))
        return rc(d, d, xs.at[i], xr.at[i], xp)

    def z_send(i):
        d = cols(f_oth, acb(i, cz))
        return rc(d, d, zs.at[i], zr.at[i], zp if i < 3 else zm)

    def z_recv(i):
        d = cols(f_oth, acb(i, 1 - cz))
        return rc(d, d, zs.at[i], zr.at[i], zp)

    def s_send(i):
        d = cols(f_oth, acb(i, cz) if i < X_CB else acb(i - X_CB, 1 - cz))
        return rc(d, d, ss.at[i], sr.at[i], sib)

    def s_recv(i):
        d = cols(f_osb, acb(i, cz) if i < X_CB else acb(i - X_CB, 1 - cz))
        return rc(d, d, ss.at[i], sr.at[i], sib)

    def o_cols(f, part):
        return WO.at[pl.ds(f * 36 + part * 9, 9)]

    def bx_send(i):
        part = cy * 2 + i
        return rc(wo.at[pl.ds(part * 9, 9)], o_cols(f_own, part), bxs.at[i], bxr.at[i], xp if i == 0 else xm)

    def bx_recv(i):
        d = o_cols(f_oth, cy * 2 + i)
        return rc(d, d, bxs.at[i], bxr.at[i], xp)

    def by_send(i):
        d = o_cols(f_oth, cy * 2 + i)
        return rc(d, d, bys.at[i], byr.at[i], yp if i == 0 else ym)

    def by_recv(i):
        d = o_cols(f_oth, (1 - cy) * 2 + i)
        return rc(d, d, bys.at[i], byr.at[i], yp)

    def bs_send(i):
        d = o_cols(f_oth, cy * 2 + i if i < 2 else (1 - cy) * 2 + i - 2)
        return rc(d, d, bss.at[i], bsr.at[i], sib)

    def bs_recv(i):
        d = o_cols(f_osb, cy * 2 + i if i < 2 else (1 - cy) * 2 + i - 2)
        return rc(d, d, bss.at[i], bsr.at[i], sib)

    sa_send = rc(wq, W.at[pl.ds(f_own * 108, 108)], ss.at[18], sr.at[18], sib)
    d_sa = W.at[pl.ds(f_sib * 108, 108)]
    sa_recv = rc(d_sa, d_sa, ss.at[18], sr.at[18], sib)
    sb_send = rc(wo, WO.at[pl.ds(f_own * 36, 36)], bss.at[4], bsr.at[4], sib)
    d_sb = WO.at[pl.ds(f_sib * 36, 36)]
    sb_recv = rc(d_sb, d_sb, bss.at[4], bsr.at[4], sib)

    def exists(name):
        dr, dc = SIDES[name]
        cond = row >= 0
        if dr < 0:
            cond = row > 0
        if dr > 0:
            cond = row < 7
        if dc < 0:
            cond = cond & (col > 0)
        if dc > 0:
            cond = cond & (col < 7)
        return cond

    src_of = dict(
        S=tok.at[pl.ds(64, 64)], N=tok.at[pl.ds(0, 64)], W=left, E=right,
        NW=left.at[pl.ds(0, 16)], SW=left.at[pl.ds(16, 16)], NE=right.at[pl.ds(0, 16)], SE=right.at[pl.ds(16, 16)],
    )

    def h_send(name):
        slot = OPPOSITE[name]
        j = NAMES.index(slot)
        return rc(src_of[name], T.at[pl.ds(*SLOT[slot])], hs.at[j], hr.at[j], tile(*SIDES[name]))

    def h_recv(name):
        j = NAMES.index(name)
        d = T.at[pl.ds(*SLOT[name])]
        return rc(d, d, hs.at[j], hr.at[j], sib)

    x_sends = [x_send(i) for i in range(X_CB)]
    for i in (0, 3, 1, 4, 2, 5):
        x_sends[i].start()
    for name in ("E", "W", "S", "N", "NW", "NE", "SW", "SE"):
        @pl.when(exists(name))
        def _():
            h_send(name).start()
    sa_send.start()
    for i in (6, 9, 7, 10, 8, 11):
        x_sends[i].start()

    def layernorm(first, count):
        def step(g, _):
            r = pl.multiple_of(first + g * 16, 16)
            v = T[pl.ds(r, 16), :].astype(jnp.float32)
            mean = jnp.sum(v, axis=1, keepdims=True) * (1.0 / 6144)
            d = v - mean
            var = jnp.sum(d * d, axis=1, keepdims=True) * (1.0 / 6144)
            n = (d * lax.rsqrt(var + 1e-06) * gain[...]).astype(jnp.bfloat16)
            for j in range(GROUPS):
                N[j, pl.ds(r, 16), :] = n[:, j * HD : (j + 1) * HD]
            return 0

        lax.fori_loop(0, count // 16, step, 0)

    def project(cb, r0, nr):
        lhs = jnp.concatenate([N[qi[cb, j], r0 : r0 + nr, :] for j in range(KEEP)], axis=1)
        w = W[pl.ds(cb * KEEP, KEEP)].reshape(KEEP * HD, HD)
        acc = jnp.dot(lhs, w, preferred_element_type=jnp.float32)
        QKV[cb, r0 : r0 + nr, :] = acc.astype(jnp.bfloat16)

    def project_range(lo, hi, r0, nr):
        def step(cb, _):
            project(cb, r0, nr)
            return 0

        lax.fori_loop(lo, hi, step, 0)

    def make_bias():
        i_q = lax.broadcasted_iota(jnp.int32, (8, ALL), 0)
        lane = lax.broadcasted_iota(jnp.int32, (8, ALL), 1)
        mid = lane < 256
        gy = lane // 16
        side = lane - 256
        side_y = (side % 64) // 4 - 4
        side_x = side % 4 + jnp.where(side < 64, -4, 16)
        ky = jnp.where(mid, jnp.where(gy >= 12, gy - 16, gy), side_y)
        kx = jnp.where(mid, lane % 16, side_x)
        gky, gkx = ky + row * TH, kx + col * TW
        inside = (gky >= 0) & (gky < 8 * TH) & (gkx >= 0) & (gkx < 8 * TW)
        for g in range(OWN // 8):
            qy, qx = g // 2, (g % 2) * 8 + i_q
            ok = inside & (jnp.abs(ky - qy) <= RADIUS) & (jnp.abs(kx - qx) <= RADIUS)

            def step(h, _):
                b = jnp.broadcast_to(base[pl.ds(h, 1), :], (8, 512))
                m = pltpu.roll(pltpu.roll(b[:, :256], (8 * g - 68) % 256, 1), 0, 1, stride=1, stride_axis=0)
                if g % 2 == 0:
                    s = pltpu.roll(b[:, 256:384], 4 * qy, 1, stride=1, stride_axis=0)
                else:
                    s = pltpu.roll(b[:, 384:512], 57 + 4 * qy, 1, stride=1, stride_axis=0)
                B[h, 8 * g : 8 * g + 8, :] = jnp.where(ok, jnp.concatenate([m, s], axis=1), NEG)
                return 0

            lax.fori_loop(0, HEADS, step, 0)

    def attend(h):
        q = QKV[h, 0:OWN, :]
        s = lax.dot_general(q, QKV[HEADS + h], (((1,), (1,)), ((), ())), preferred_element_type=jnp.float32)
        s = s * (HD ** -0.5) + B[h]
        m = jnp.max(s, axis=1, keepdims=True)
        p = jnp.exp(s - m)
        total = jnp.sum(p, axis=1, keepdims=True)
        o = jnp.dot(p.astype(jnp.bfloat16), QKV[2 * HEADS + h], preferred_element_type=jnp.float32)
        ATT[h] = (o / total).astype(jnp.bfloat16)

    def output(cb):
        lhs = jnp.concatenate([ATT[oi[cb, j]] for j in range(KEEP_O)], axis=1)
        w = WO[pl.ds(cb * KEEP_O, KEEP_O)].reshape(KEEP_O * HD, HD)
        acc = jnp.dot(lhs, w, preferred_element_type=jnp.float32)
        lanes = pl.ds(pl.multiple_of(cb * HD, HD), HD)
        out[:, lanes] = (acc + T[0:OWN, lanes].astype(jnp.float32)).astype(jnp.bfloat16)

    c_tok.wait()
    layernorm(0, OWN)
    for i in (0, 3):
        x_recv(i).wait_recv()
        z_send(i).start()
        s_send(i).start()
    make_bias()
    for i in (1, 4, 2, 5):
        x_recv(i).wait_recv()
        z_send(i).start()
        s_send(i).start()
    c_wq.wait()
    project_range(f_own * SHARD, f_own * SHARD + SHARD, 0, OWN)
    sa_recv.wait_recv()
    project_range(f_sib * SHARD, f_sib * SHARD + SHARD, 0, OWN)

    for i in (6, 9, 7, 10, 8, 11):
        x_recv(i).wait_recv()
        s_send(i).start()
    bx_sends = [bx_send(i) for i in range(2)]
    for c in bx_sends:
        c.start()
    sb_send.start()

    for name in NAMES:
        first, count = SLOT[name]

        @pl.when(exists(name))
        def _():
            h_recv(name).wait_recv()

        @pl.when(jnp.logical_not(exists(name)))
        def _():
            T[first : first + count, :] = jnp.zeros((count, 6144), jnp.bfloat16)

    layernorm(OWN, ALL - OWN)

    for i in range(Z_CB):
        z_recv(i).wait_recv()
        s_send(X_CB + i).start()

    project_range(f_oth * SHARD, f_oth * SHARD + SHARD, 0, OWN)
    for i in range(2):
        bx_recv(i).wait_recv()
        by_send(i).start()
        bs_send(i).start()
    for i in range(18):
        s_recv(i).wait_recv()
    project_range(f_osb * SHARD, f_osb * SHARD + SHARD, 0, OWN)
    project_range(HEADS, 3 * HEADS, OWN, ALL - OWN)

    for i in range(2):
        by_recv(i).wait_recv()
        bs_send(2 + i).start()

    def head(h, _):
        attend(h)
        return 0

    lax.fori_loop(0, HEADS, head, 0)

    c_wo.wait()
    sb_recv.wait_recv()
    for i in range(4):
        bs_recv(i).wait_recv()

    def column(cb, _):
        output(cb)
        return 0

    lax.fori_loop(0, GROUPS, column, 0)

    for c in x_sends + bx_sends + [sa_send, sb_send]:
        c.wait_send()
    for i in range(Z_CB):
        z_send(i).wait_send()
    for i in range(18):
        s_send(i).wait_send()
    for i in range(2):
        by_send(i).wait_send()
    for i in range(4):
        bs_send(i).wait_send()
    for name in NAMES:
        @pl.when(exists(name))
        def _():
            h_send(name).wait_send()


def body(tokens, ln_gain, qkv_blocks, qkv_index, out_blocks, out_index, rel_bias):
    tile = tokens[0]
    left = tile[:, :RADIUS].reshape(TH * RADIUS, -1)
    right = tile[:, TW - RADIUS :].reshape(TH * RADIUS, -1)
    square = rel_bias.reshape(HEADS, 9, 9)
    mid = jnp.pad(square, ((0, 0), (0, 0), (0, 7))).reshape(HEADS, 144)
    mid = jnp.pad(mid, ((0, 0), (0, 112)))
    west = jnp.pad(square[:, :, :4].reshape(HEADS, 36), ((0, 0), (0, 92)))
    east = jnp.pad(square[:, :, 5:].reshape(HEADS, 36), ((0, 0), (0, 92)))
    base = jnp.concatenate([mid, west, east], axis=1)
    any_, vmem, smem = pl.BlockSpec(memory_space=pl.ANY), pl.BlockSpec(memory_space=pltpu.VMEM), pl.BlockSpec(memory_space=pltpu.SMEM)
    dma = lambda n: pltpu.SemaphoreType.DMA((n,))
    bf = jnp.bfloat16
    mixed = pl.pallas_call(
        kernel,
        out_shape=jax.ShapeDtypeStruct((OWN, 6144), bf),
        in_specs=[smem, smem, any_, any_, any_, vmem, vmem, any_, any_],
        out_specs=vmem,
        scratch_shapes=[
            pltpu.VMEM((ALL, 6144), bf),
            pltpu.VMEM((GROUPS, ALL, HD), bf),
            pltpu.VMEM((432, HD, HD), bf),
            pltpu.VMEM((144, HD, HD), bf),
            pltpu.VMEM((72, ALL, HD), bf),
            pltpu.VMEM((HEADS, OWN, HD), bf),
            pltpu.VMEM((HEADS, OWN, ALL), jnp.float32),
            dma(3), dma(8), dma(8), dma(12), dma(12), dma(6), dma(6), dma(19), dma(19),
            dma(2), dma(2), dma(2), dma(2), dma(5), dma(5),
        ],
        compiler_params=pltpu.CompilerParams(collective_id=0, has_side_effects=True, vmem_limit_bytes=58 * 2**20),
        cost_estimate=pl.CostEstimate(flops=6 * 10**9, bytes_accessed=30 * 2**20, transcendentals=10**6),
        name="block",
    )(
        qkv_index, out_index, tile.reshape(OWN, -1), left, right, ln_gain.reshape(1, -1), base,
        qkv_blocks.reshape(SHARD * KEEP, HD, HD), out_blocks.reshape(SHARD_O * KEEP_O, HD, HD),
    )
    return mixed.reshape(1, TH, TW, -1)


def solution(mesh):
    in_specs = (
        P("fsdp", "row", "col", None),
        P(),
        P("fsdp", None, None, None),
        P(),
        P("fsdp", None, None, None),
        P(),
        P(),
    )
    out_specs = P("fsdp", "row", "col", None)
    return jax.shard_map(body, mesh=mesh, in_specs=in_specs, out_specs=out_specs, check_vma=False)
```

```python
import jax
import jax.numpy as jnp
from jax import lax
from jax.experimental import pallas as pl
from jax.experimental.pallas import tpu as pltpu
from jax.sharding import PartitionSpec as P

MESH = pl.DeviceIdType.MESH
HD = 128
HEADS = 24
KEEP = 6
KEEP_O = 3
RADIUS = 4
TH, TW = 8, 16
OWN = TH * TW
ALL = (TH + 2 * RADIUS) * (TW + 2 * RADIUS)
PAIR = 256
GROUPS = 48
SHARD = 18
SHARD_O = 12
NEG = -1e30
STAGES = ("X1", "X2", "Y1", "Y2", "Z1", "Z2")


def kernel(
    qi, oi, tok, gain, base, wq, wo, out,
    NAT, T, N, NO, W, WO, Q, KV, ATT, B, EDGE,
    loc, hs, hr, ws, wr, ss, sr, bs, br, bss, bsr, os, orr,
):
    row, col, fs_ = lax.axis_index("row"), lax.axis_index("col"), lax.axis_index("fsdp")
    x, y, z, k = (row // 4) * 2 + fs_ // 2, row % 4, col, fs_ % 2

    def dev(dx, dy, dz, dk):
        xx, yy, zz, kk = (x + dx) % 4, (y + dy) % 4, (z + dz) % 8, (k + dk) % 2
        return ((xx // 2) * 4 + yy, zz, (xx % 2) * 2 + kk)

    def tile(dr, dc):
        return ((row + dr + 8) % 8, (col + dc + 8) % 8, fs_)

    f_own = fs_
    f_sib = (x % 2) * 2 + (1 - k)
    f_oth = (1 - x % 2) * 2 + k
    f_osb = (1 - x % 2) * 2 + (1 - k)
    cz, cy = z % 2, y % 2
    sib = dev(0, 0, 0, 1)
    xp, xm = dev(1, 0, 0, 0), dev(3, 0, 0, 0)
    yp, ym = dev(0, 1, 0, 0), dev(0, 3, 0, 0)
    zp, zm = dev(0, 0, 1, 0), dev(0, 0, 7, 0)
    chunk_of = dict(
        X1=cy, X2=2 + 2 * cy + cz, Y1=1 - cy, Y2=2 + 2 * (1 - cy) + cz, Z1=2 + 2 * cy + 1 - cz, Z2=2 + 2 * (1 - cy) + 1 - cz
    )

    c_tok = pltpu.make_async_copy(tok, NAT, loc.at[0])
    c_wq = pltpu.make_async_copy(wq, W.at[pl.ds(f_own * 108, 108)], loc.at[1])
    c_wo = pltpu.make_async_copy(wo, WO.at[pl.ds(f_own * 36, 36)], loc.at[2])
    c_tok.start()
    c_wq.start()
    c_wo.start()

    partners = [sib, xp, xm, yp, ym, zp, zm, tile(1, 0), tile(-1, 0)]
    barrier = pltpu.get_barrier_semaphore()
    for p in partners:
        pl.semaphore_signal(barrier, inc=1, device_id=p, device_id_type=MESH)
    pl.semaphore_wait(barrier, len(partners))

    def rc(src, dst, s, r, to):
        return pltpu.make_async_remote_copy(src_ref=src, dst_ref=dst, send_sem=s, recv_sem=r, device_id=to, device_id_type=MESH)

    def a_ref(f, stage, sub):
        return W.at[pl.ds(((f * 6 + chunk_of[stage]) * 3 + sub) * KEEP, KEEP)]

    def o_ref(f, stage):
        return WO.at[pl.ds((f * 6 + chunk_of[stage]) * 6, 6)]

    def a_first(stage, sub, to):
        j = STAGES.index(stage) * 3 + sub
        src = wq.at[pl.ds((chunk_of[stage] * 3 + sub) * KEEP, KEEP)]
        return rc(src, a_ref(f_own, stage, sub), ws.at[j], wr.at[j], to)

    def a_forward(have, stage, sub, to):
        j = STAGES.index(stage) * 3 + sub
        d = a_ref(f_oth, have, sub)
        return rc(d, d, ws.at[j], wr.at[j], to)

    def a_recv(stage, sub):
        j = STAGES.index(stage) * 3 + sub
        d = a_ref(f_oth, stage, sub)
        return rc(d, d, ws.at[j], wr.at[j], sib)

    def s_send(stage, sub):
        j = STAGES.index(stage) * 3 + sub
        d = a_ref(f_oth, stage, sub)
        return rc(d, d, ss.at[j], sr.at[j], sib)

    def s_recv(stage, sub):
        j = STAGES.index(stage) * 3 + sub
        d = a_ref(f_osb, stage, sub)
        return rc(d, d, ss.at[j], sr.at[j], sib)

    def o_first(stage, to):
        j = STAGES.index(stage)
        return rc(wo.at[pl.ds(chunk_of[stage] * 6, 6)], o_ref(f_own, stage), bs.at[j], br.at[j], to)

    def o_forward(have, stage, to):
        j = STAGES.index(stage)
        d = o_ref(f_oth, have)
        return rc(d, d, bs.at[j], br.at[j], to)

    def o_recv(stage):
        j = STAGES.index(stage)
        d = o_ref(f_oth, stage)
        return rc(d, d, bs.at[j], br.at[j], sib)

    def os_send(stage):
        j = STAGES.index(stage)
        d = o_ref(f_oth, stage)
        return rc(d, d, bss.at[j], bsr.at[j], sib)

    def os_recv(stage):
        j = STAGES.index(stage)
        d = o_ref(f_osb, stage)
        return rc(d, d, bss.at[j], bsr.at[j], sib)

    sa_send = rc(wq, W.at[pl.ds(f_own * 108, 108)], os.at[0], orr.at[0], sib)
    d_sa = W.at[pl.ds(f_sib * 108, 108)]
    sa_recv = rc(d_sa, d_sa, os.at[0], orr.at[0], sib)
    sb_send = rc(wo, WO.at[pl.ds(f_own * 36, 36)], os.at[1], orr.at[1], sib)
    d_sb = WO.at[pl.ds(f_sib * 36, 36)]
    sb_recv = rc(d_sb, d_sb, os.at[1], orr.at[1], sib)

    up, down, west, east = row > 0, row < 7, col > 0, col < 7
    four = pl.ds(1, 4)
    halo = dict(
        N=((four, pl.ds(32, 16)), (four, pl.ds(0, 16)), tile(1, 0), down, up),
        S=((four, pl.ds(16, 16)), (four, pl.ds(48, 16)), tile(-1, 0), up, down),
        W=((4, pl.ds(16, 32)), (0, pl.ds(16, 32)), tile(0, 1), east, west),
        E=((1, pl.ds(16, 32)), (5, pl.ds(16, 32)), tile(0, -1), west, east),
        NW=((4, pl.ds(0, 16)), (0, pl.ds(0, 16)), tile(0, 1), up & east, up & west),
        NE=((1, pl.ds(0, 16)), (5, pl.ds(0, 16)), tile(0, -1), up & west, up & east),
        SW=((4, pl.ds(48, 16)), (0, pl.ds(48, 16)), tile(0, 1), down & east, down & west),
        SE=((1, pl.ds(48, 16)), (5, pl.ds(48, 16)), tile(0, -1), down & west, down & east),
    )
    names = tuple(halo)

    def h_copy(name):
        src, dst, to, _, _ = halo[name]
        j = names.index(name)
        return rc(T.at[src], T.at[dst], hs.at[j], hr.at[j], to)

    def h_start(*which):
        for name in which:
            @pl.when(halo[name][3])
            def _():
                h_copy(name).start()

    def h_wait_send(*which):
        for name in which:
            @pl.when(halo[name][3])
            def _():
                h_copy(name).wait_send()

    def h_wait(*which):
        for name in which:
            d = T.at[halo[name][1]]
            j = names.index(name)

            @pl.when(halo[name][4])
            def _():
                rc(d, d, hs.at[j], hr.at[j], sib).wait_recv()

    a_starts = [a_first(s, i, to) for i in range(3) for s, to in (("X1", xp), ("X2", xm))]
    for c in a_starts:
        c.start()
    sa_send.start()

    def swap_fours(a, b):
        low = lax.broadcasted_iota(jnp.int32, a.shape, 0) < 4
        return jnp.where(low, a, pltpu.roll(b, 4, 0)), jnp.where(low, pltpu.roll(a, 4, 0), b)

    def regroup():
        def step(i, _):
            lanes = pl.ds(pl.multiple_of(i * 256, 256), 256)
            for jj in range(2):
                v = NAT[pl.ds(64 * jj, 64), lanes].astype(jnp.float32)
                for half in range(2):
                    pairs = [swap_fours(v[32 * j + 8 * half : 32 * j + 8 * half + 8], v[32 * j + 16 + 8 * half : 32 * j + 24 + 8 * half]) for j in range(2)]
                    for e in range(2):
                        t = jnp.concatenate([pairs[0][e], pairs[1][e]], axis=0)
                        T[1 + 2 * half + e, 16 + 16 * jj : 32 + 16 * jj, lanes] = t.astype(jnp.bfloat16)
            return 0

        lax.fori_loop(0, 24, step, 0)

    def norm_rows(g, r, own_row=None):
        v = T[g, pl.ds(r, 16), :].astype(jnp.float32)
        mean = jnp.sum(v, axis=1, keepdims=True) * (1.0 / 6144)
        d = v - mean
        var = jnp.sum(d * d, axis=1, keepdims=True) * (1.0 / 6144)
        n = (d * lax.rsqrt(var + 1e-06) * gain[...]).astype(jnp.bfloat16)
        at = pl.multiple_of(g * 64 + r, 16)
        for j in range(GROUPS):
            N[j, pl.ds(at, 16), :] = n[:, j * HD : (j + 1) * HD]
            if own_row is not None:
                NO[j, pl.ds(own_row, 16), :] = n[:, j * HD : (j + 1) * HD]

    def norm_own():
        def step(i, _):
            g, half = i // 2, i % 2
            norm_rows(1 + g, pl.multiple_of(16 + 16 * half, 16), pl.multiple_of(16 * i, 16))
            return 0

        lax.fori_loop(0, 8, step, 0)

    def norm_vertical():
        def step(i, _):
            norm_rows(1 + i // 2, pl.multiple_of(48 * (i % 2), 16))
            return 0

        lax.fori_loop(0, 8, step, 0)

    def norm_sides():
        def step(i, _):
            norm_rows(5 * (i // 4), pl.multiple_of(16 * (i % 4), 16))
            return 0

        lax.fori_loop(0, 8, step, 0)

    def rows_of(ref, cb, part):
        cols = []
        for j in range(KEEP):
            i = qi[cb, j]
            if part == "sides":
                cols.append(jnp.concatenate([ref[i, 0:64, :], ref[i, 320:384, :]], axis=0))
            elif part in ("middle", "both"):
                cols.append(ref[i, 64:320, :])
            else:
                cols.append(ref[i])
        return jnp.concatenate(cols, axis=1)

    def project(ref, cb, part):
        w = W[pl.ds(cb * KEEP, KEEP)].reshape(KEEP * HD, HD)
        return jnp.dot(rows_of(ref, cb, part), w, preferred_element_type=jnp.float32).astype(jnp.bfloat16)

    def chunk(c, part):
        lo = c * 3

        @pl.when(c < HEADS // 3)
        def _():
            if part in ("own", "both", "all"):
                for e in range(3):
                    Q[lo + e] = project(NO, lo + e, "own")

        @pl.when(c >= HEADS // 3)
        def _():
            if part == "own":
                return
            for e in range(3):
                r = project(N, lo + e, part)
                if part in ("middle", "both"):
                    KV[lo + e - HEADS, 64:320, :] = r
                elif part == "sides":
                    KV[lo + e - HEADS, 0:64, :] = r[0:64]
                    KV[lo + e - HEADS, 320:384, :] = r[64:128]
                else:
                    KV[lo + e - HEADS] = r

    def shard(f, part, first=0, last=6):
        def step(c, _):
            chunk(f * 6 + c, part)
            return 0

        lax.fori_loop(first, last, step, 0)

    def make_bias():
        lane = lax.broadcasted_iota(jnp.int32, (8, PAIR), 1)
        sub = lax.broadcasted_iota(jnp.int32, (8, PAIR), 0)
        ky, kx = (lane % 64) // 4 - 4, (lane // 64) * 4 + lane % 4 - 4
        inside = (ky + row * TH >= 0) & (ky + row * TH < 8 * TH)
        low = lax.broadcasted_iota(jnp.int32, (8, HD), 1) < 64
        right = lax.broadcasted_iota(jnp.int32, (8, HD), 1) % 4 >= lax.broadcasted_iota(jnp.int32, (8, HD), 0) % 4
        for i in range(4):
            qy, qx = 2 * i + sub // 4, sub % 4
            ok = inside & (jnp.abs(ky - qy) <= RADIUS) & (jnp.abs(kx - qx) <= RADIUS)

            def step(h, _):
                b = jnp.broadcast_to(base[pl.ds(h, 1), :], (8, 512))
                r = [pltpu.roll(b[:, 128 * e : 128 * e + 128], 8 * i, 1, stride=1, stride_axis=0) for e in range(4)]
                same = jnp.where(right, r[2], r[1])
                first = jnp.where(ok[:, :HD], jnp.where(low, r[0], pltpu.roll(same, 64, 1)), NEG)
                last = jnp.where(ok[:, HD:], r[3], NEG)
                turned = pltpu.roll(first, 64, 1)
                B[h, 8 * i : 8 * i + 8, :] = jnp.concatenate([first, jnp.where(low, last, NEG)], axis=1)
                B[h, 32 + 8 * i : 40 + 8 * i, :] = jnp.concatenate([jnp.where(low, NEG, turned), jnp.where(low, turned, pltpu.roll(last, 64, 1))], axis=1)
                return 0

            lax.fori_loop(0, HEADS, step, 0, unroll=4)
        wide = lax.broadcasted_iota(jnp.int32, (8, PAIR), 1)
        EDGE[0] = jnp.where((wide < 64) & (col == 0), NEG, 0.0)
        EDGE[1] = jnp.where((wide >= 192) & (col == 7), NEG, 0.0)

    def attend(h):
        kk, vv, qq, bias = KV[h], KV[HEADS + h], Q[h], B[h]
        outs = []
        for p in range(2):
            s = lax.dot_general(
                qq[64 * p : 64 * p + 64], kk[128 * p : 128 * p + PAIR], (((1,), (1,)), ((), ())), preferred_element_type=jnp.float32
            )
            s = s * (HD ** -0.5) + bias + EDGE[p, 0:1, :]
            m = jnp.max(s, axis=1, keepdims=True)
            w = jnp.exp(s - m)
            total = jnp.sum(w, axis=1, keepdims=True)
            o = jnp.dot(w.astype(jnp.bfloat16), vv[128 * p : 128 * p + PAIR], preferred_element_type=jnp.float32) / total
            outs += [o[0:32], o[32:64]]
        for j in range(4):
            halves = []
            for half in range(2):
                halves.append(swap_fours(outs[2 * half][8 * j : 8 * j + 8], outs[2 * half + 1][8 * j : 8 * j + 8]))
            for e in range(2):
                ATT[h, 32 * j + 16 * e : 32 * j + 16 * e + 16, :] = jnp.concatenate([halves[0][e], halves[1][e]], axis=0).astype(jnp.bfloat16)

    def output(cb):
        lhs = jnp.concatenate([ATT[oi[cb, j]] for j in range(KEEP_O)], axis=1)
        w = WO[pl.ds(cb * KEEP_O, KEEP_O)].reshape(KEEP_O * HD, HD)
        acc = jnp.dot(lhs, w, preferred_element_type=jnp.float32)
        lanes = pl.ds(pl.multiple_of(cb * HD, HD), HD)
        out[:, lanes] = (acc + NAT[:, lanes].astype(jnp.float32)).astype(jnp.bfloat16)

    c_tok.wait()
    regroup()
    h_start("N", "S", "W", "E")

    @pl.when(jnp.logical_not(up))
    def _():
        T[:, 0:16, :] = jnp.zeros((6, 16, 6144), jnp.bfloat16)

    @pl.when(jnp.logical_not(down))
    def _():
        T[:, 48:64, :] = jnp.zeros((6, 16, 6144), jnp.bfloat16)

    @pl.when(jnp.logical_not(west))
    def _():
        T[0] = jnp.zeros((64, 6144), jnp.bfloat16)

    @pl.when(jnp.logical_not(east))
    def _():
        T[5] = jnp.zeros((64, 6144), jnp.bfloat16)

    def pump_x(sub):
        for s in ("X1", "X2"):
            a_recv(s, sub).wait_recv()
        a_forward("X2", "Z1", sub, zp).start()
        a_forward("X2", "Y2", sub, ym).start()
        a_forward("X1", "Y1", sub, yp).start()
        s_send("X1", sub).start()
        s_send("X2", sub).start()

    def pump_yz(sub):
        for s in ("Y2", "Y1", "Z1"):
            a_recv(s, sub).wait_recv()
            if s == "Y2":
                a_forward("Y2", "Z2", sub, zm).start()
            s_send(s, sub).start()

    norm_own()
    pump_x(0)
    make_bias()
    pump_x(1)
    c_wq.wait()
    shard(f_own, "own")
    sa_recv.wait_recv()
    shard(f_sib, "own")
    pump_x(2)
    o_starts = [o_first("X1", xp), o_first("X2", xm)]
    for c in o_starts:
        c.start()
    sb_send.start()

    h_wait("N", "S")
    h_start("NW", "NE", "SW", "SE")
    norm_vertical()
    pump_yz(0)
    shard(f_own, "middle")
    pump_yz(1)
    shard(f_sib, "middle")
    pump_yz(2)

    def received(s, part):
        chunk(f_oth * 6 + chunk_of[s], part)
        for i in range(3):
            s_recv(s, i).wait_recv()
        chunk(f_osb * 6 + chunk_of[s], part)

    def again(s):
        chunk(f_oth * 6 + chunk_of[s], "sides")
        chunk(f_osb * 6 + chunk_of[s], "sides")

    for s in ("X1", "X2"):
        received(s, "both")
    for s in ("X1", "X2"):
        o_recv(s).wait_recv()
        os_send(s).start()
    o_forward("X2", "Z1", zp).start()
    o_forward("X2", "Y2", ym).start()
    o_forward("X1", "Y1", yp).start()
    h_wait("W", "E", "NW", "NE", "SW", "SE")
    norm_sides()
    for i in range(3):
        a_recv("Z2", i).wait_recv()
        s_send("Z2", i).start()
    for s in ("Y2", "Y1", "Z1"):
        o_recv(s).wait_recv()
        os_send(s).start()
        if s == "Y2":
            o_forward("Y2", "Z2", zm).start()
    shard(f_own, "sides")
    shard(f_sib, "sides")
    for s in ("X1", "X2"):
        again(s)
    for s in ("Y1", "Y2", "Z1", "Z2"):
        received(s, "all")

    def head(h, _):
        attend(h)
        return 0

    lax.fori_loop(0, HEADS, head, 0, unroll=2)

    o_recv("Z2").wait_recv()
    os_send("Z2").start()
    c_wo.wait()
    sb_recv.wait_recv()
    for s in STAGES:
        os_recv(s).wait_recv()

    def column(cb, _):
        output(cb)
        return 0

    lax.fori_loop(0, GROUPS, column, 0, unroll=4)

    for c in a_starts + o_starts + [sa_send, sb_send]:
        c.wait_send()
    for have, s, to in (("X2", "Z1", zp), ("X2", "Y2", ym), ("X1", "Y1", yp), ("Y2", "Z2", zm)):
        for i in range(3):
            a_forward(have, s, i, to).wait_send()
        o_forward(have, s, to).wait_send()
    for s in STAGES:
        for i in range(3):
            s_send(s, i).wait_send()
        os_send(s).wait_send()
    h_wait_send(*names)


def body(tokens, ln_gain, qkv_blocks, qkv_index, out_blocks, out_index, rel_bias):
    square = rel_bias.reshape(HEADS, 9, 9)
    wide = lambda cols: jnp.pad(square[:, :, cols : cols + 4].reshape(HEADS, 36), ((0, 0), (0, HD - 36)))
    base = jnp.concatenate([wide(0), jnp.roll(wide(0), -4, axis=1), wide(4), jnp.roll(wide(5), -3, axis=1)], axis=1)
    any_, vmem, smem = pl.BlockSpec(memory_space=pl.ANY), pl.BlockSpec(memory_space=pltpu.VMEM), pl.BlockSpec(memory_space=pltpu.SMEM)
    dma = lambda n: pltpu.SemaphoreType.DMA((n,))
    bf = jnp.bfloat16
    mixed = pl.pallas_call(
        kernel,
        out_shape=jax.ShapeDtypeStruct((OWN, 6144), bf),
        in_specs=[smem, smem, any_, vmem, vmem, any_, any_],
        out_specs=vmem,
        scratch_shapes=[
            pltpu.VMEM((OWN, 6144), bf),
            pltpu.VMEM((6, 64, 6144), bf),
            pltpu.VMEM((GROUPS, ALL, HD), bf),
            pltpu.VMEM((GROUPS, OWN, HD), bf),
            pltpu.VMEM((432, HD, HD), bf),
            pltpu.VMEM((144, HD, HD), bf),
            pltpu.VMEM((HEADS, OWN, HD), bf),
            pltpu.VMEM((2 * HEADS, ALL, HD), bf),
            pltpu.VMEM((HEADS, OWN, HD), bf),
            pltpu.VMEM((HEADS, 64, PAIR), jnp.float32),
            pltpu.VMEM((2, 8, PAIR), jnp.float32),
            dma(3), dma(8), dma(8), dma(18), dma(18), dma(18), dma(18), dma(6), dma(6), dma(6), dma(6), dma(2), dma(2),
        ],
        compiler_params=pltpu.CompilerParams(collective_id=0, has_side_effects=True, vmem_limit_bytes=58 * 2**20),
        cost_estimate=pl.CostEstimate(flops=6 * 10**9, bytes_accessed=30 * 2**20, transcendentals=10**6),
        name="block",
    )(
        qkv_index, out_index, tokens.reshape(OWN, -1), ln_gain.reshape(1, -1), base,
        qkv_blocks.reshape(SHARD * KEEP, HD, HD), out_blocks.reshape(SHARD_O * KEEP_O, HD, HD),
    )
    return mixed.reshape(1, TH, TW, -1)


def solution(mesh):
    in_specs = (
        P("fsdp", "row", "col", None),
        P(),
        P("fsdp", None, None, None),
        P(),
        P("fsdp", None, None, None),
        P(),
        P(),
    )
    out_specs = P("fsdp", "row", "col", None)
    return jax.shard_map(body, mesh=mesh, in_specs=in_specs, out_specs=out_specs, check_vma=False)
```

```python
import jax
import jax.numpy as jnp
from jax import lax
from jax.experimental import pallas as pl
from jax.experimental.pallas import tpu as pltpu
from jax.sharding import PartitionSpec as P

MESH = pl.DeviceIdType.MESH
HD = 128
HEADS = 24
KEEP = 6
KEEP_O = 3
RADIUS = 4
TH, TW = 8, 16
OWN = TH * TW
ALL = (TH + 2 * RADIUS) * (TW + 2 * RADIUS)
PAIR = 256
GROUPS = 48
SHARD = 18
SHARD_O = 12
NEG = -1e30


def kernel(
    qi_any, oi_any, tok, gain, rel, wq, wo, out,
    NAT, T, N, NO, W, WO, Q, KV, ATT, B, EDGE, SHIFT, QI, OI,
    loc, hs, hr, ws, wr, ss, sr, bs, br, bss, bsr, os, orr,
):
    row, col, fs_ = lax.axis_index("row"), lax.axis_index("col"), lax.axis_index("fsdp")
    x, y, z, k = (row // 4) * 2 + fs_ // 2, row % 4, col, fs_ % 2

    def dev(dx, dy, dz, dk):
        xx, yy, zz, kk = (x + dx) % 4, (y + dy) % 4, (z + dz) % 8, (k + dk) % 2
        return ((xx // 2) * 4 + yy, zz, (xx % 2) * 2 + kk)

    def tile(dr, dc):
        return ((row + dr + 8) % 8, (col + dc + 8) % 8, fs_)

    f_own = fs_
    f_sib = (x % 2) * 2 + (1 - k)
    f_oth = (1 - x % 2) * 2 + k
    f_osb = (1 - x % 2) * 2 + (1 - k)
    cz, cy = z % 2, y % 2
    sib = dev(0, 0, 0, 1)
    xp, xm = dev(1, 0, 0, 0), dev(3, 0, 0, 0)
    yp, ym = dev(0, 1, 0, 0), dev(0, 3, 0, 0)
    zp, zm = dev(0, 0, 1, 0), dev(0, 0, 7, 0)
    ya, yb, za, zb = 4 * cy, 4 * (1 - cy), 8 + 4 * cz, 8 + 4 * (1 - cz)
    came = [ya + i for i in range(4)] + [za + i for i in range(4)] + [16, 17] + [yb + i for i in range(4)] + [zb + i for i in range(4)]

    c_qi = pltpu.make_async_copy(qi_any, QI, loc.at[3])
    c_oi = pltpu.make_async_copy(oi_any, OI, loc.at[4])
    c_qi.start()
    c_oi.start()
    c_tok = pltpu.make_async_copy(tok, NAT, loc.at[0])
    c_wq = pltpu.make_async_copy(wq, W.at[pl.ds(f_own * 108, 108)], loc.at[1])
    c_wo = pltpu.make_async_copy(wo, WO.at[pl.ds(f_own * 36, 36)], loc.at[2])
    c_tok.start()
    c_wq.start()
    c_wo.start()

    partners = [sib, xp, xm, yp, ym, zp, zm, tile(1, 0), tile(-1, 0), dev(2, 0, 0, 0)]
    barrier = pltpu.get_barrier_semaphore()
    for p in partners:
        pl.semaphore_signal(barrier, inc=1, device_id=p, device_id_type=MESH)
    pl.semaphore_wait(barrier, len(partners))

    def rc(src, dst, s, r, to):
        return pltpu.make_async_remote_copy(src_ref=src, dst_ref=dst, send_sem=s, recv_sem=r, device_id=to, device_id_type=MESH)

    def a_ref(f, j):
        return W.at[pl.ds((f * SHARD + came[j]) * KEEP, KEEP)]

    def a_first(j):
        src = wq.at[pl.ds(came[j] * KEEP, KEEP)]
        return rc(src, a_ref(f_own, j), ws.at[j], wr.at[j], xp if j < 4 or j == 8 else xm)

    def a_forward(j):
        d = a_ref(f_oth, j)
        to = (yp, ym, zp, zm)[(j // 4) * 2 + j % 2]
        return rc(d, d, ws.at[10 + j], wr.at[10 + j], to)

    def a_recv(j):
        d = a_ref(f_oth, j)
        return rc(d, d, ws.at[j], wr.at[j], sib)

    def s_send(j):
        d = a_ref(f_oth, j)
        return rc(d, d, ss.at[j], sr.at[j], sib)

    def s_recv(j):
        d = a_ref(f_osb, j)
        return rc(d, d, ss.at[j], sr.at[j], sib)

    parts = [cy, 2 + cz, 1 - cy, 2 + 1 - cz]

    def o_ref(f, j):
        return WO.at[pl.ds(f * 36 + parts[j] * 9, 9)]

    def o_first(j):
        return rc(wo.at[pl.ds(parts[j] * 9, 9)], o_ref(f_own, j), bs.at[j], br.at[j], (xp, xm)[j])

    def o_forward(j):
        d = o_ref(f_oth, j)
        return rc(d, d, bs.at[2 + j], br.at[2 + j], (yp, zp)[j])

    def o_recv(j):
        d = o_ref(f_oth, j)
        return rc(d, d, bs.at[j], br.at[j], sib)

    def os_send(j):
        d = o_ref(f_oth, j)
        return rc(d, d, bss.at[j], bsr.at[j], sib)

    def os_recv(j):
        d = o_ref(f_osb, j)
        return rc(d, d, bss.at[j], bsr.at[j], sib)

    sa_send = rc(wq, W.at[pl.ds(f_own * 108, 108)], os.at[0], orr.at[0], sib)
    d_sa = W.at[pl.ds(f_sib * 108, 108)]
    sa_recv = rc(d_sa, d_sa, os.at[0], orr.at[0], sib)
    sb_send = rc(wo, WO.at[pl.ds(f_own * 36, 36)], os.at[1], orr.at[1], sib)
    d_sb = WO.at[pl.ds(f_sib * 36, 36)]
    sb_recv = rc(d_sb, d_sb, os.at[1], orr.at[1], sib)

    up, down, west, east = row > 0, row < 7, col > 0, col < 7
    four, low2, high2, across = pl.ds(1, 4), pl.ds(1, 2), pl.ds(3, 2), dev(2, 0, 0, 0)
    halo = dict(
        N=((four, pl.ds(32, 16)), (four, pl.ds(0, 16)), tile(1, 0), down & (row != 3), up & (row != 4)),
        S=((four, pl.ds(16, 16)), (four, pl.ds(48, 16)), tile(-1, 0), up & (row != 4), down & (row != 3)),
        W=((4, pl.ds(16, 32)), (0, pl.ds(16, 32)), tile(0, 1), east, west),
        E=((1, pl.ds(16, 32)), (5, pl.ds(16, 32)), tile(0, -1), west, east),
        NW=((4, pl.ds(0, 16)), (0, pl.ds(0, 16)), tile(0, 1), up & east, up & west),
        NE=((1, pl.ds(0, 16)), (5, pl.ds(0, 16)), tile(0, -1), up & west, up & east),
        SW=((4, pl.ds(48, 16)), (0, pl.ds(48, 16)), tile(0, 1), down & east, down & west),
        SE=((1, pl.ds(48, 16)), (5, pl.ds(48, 16)), tile(0, -1), down & west, down & east),
        ND=((low2, pl.ds(32, 16)), (low2, pl.ds(0, 16)), tile(1, 0), row == 3, row == 4),
        NR=((high2, pl.ds(32, 16)), (high2, pl.ds(0, 16)), yp, row == 3, row == 0),
        NF=((high2, pl.ds(0, 16)), (high2, pl.ds(0, 16)), across, row == 0, row == 4),
        SD=((low2, pl.ds(16, 16)), (low2, pl.ds(48, 16)), tile(-1, 0), row == 4, row == 3),
        SR=((high2, pl.ds(16, 16)), (high2, pl.ds(48, 16)), ym, row == 4, row == 7),
        SF=((high2, pl.ds(48, 16)), (high2, pl.ds(48, 16)), across, row == 7, row == 3),
    )
    names = tuple(halo)

    def h_copy(name):
        src, dst, to, _, _ = halo[name]
        j = names.index(name)
        return rc(T.at[src], T.at[dst], hs.at[j], hr.at[j], to)

    def h_start(*which):
        for name in which:
            @pl.when(halo[name][3])
            def _():
                h_copy(name).start()

    def h_wait_send(*which):
        for name in which:
            @pl.when(halo[name][3])
            def _():
                h_copy(name).wait_send()

    def h_wait(*which):
        for name in which:
            d = T.at[halo[name][1]]
            j = names.index(name)

            @pl.when(halo[name][4])
            def _():
                rc(d, d, hs.at[j], hr.at[j], sib).wait_recv()

    a_starts = [a_first(j) for j in (0, 4, 1, 5, 2, 6, 3, 7, 8, 9)]
    for c in a_starts:
        c.start()
    sa_send.start()

    def swap_fours(a, b):
        low = lax.broadcasted_iota(jnp.int32, a.shape, 0) < 4
        return jnp.where(low, a, pltpu.roll(b, 4, 0)), jnp.where(low, pltpu.roll(a, 4, 0), b)

    def regroup():
        def step(i, _):
            lanes = pl.ds(pl.multiple_of(i * 256, 256), 256)
            for jj in range(2):
                v = NAT[pl.ds(64 * jj, 64), lanes].astype(jnp.float32)
                for half in range(2):
                    pairs = [swap_fours(v[32 * j + 8 * half : 32 * j + 8 * half + 8], v[32 * j + 16 + 8 * half : 32 * j + 24 + 8 * half]) for j in range(2)]
                    for e in range(2):
                        t = jnp.concatenate([pairs[0][e], pairs[1][e]], axis=0)
                        T[1 + 2 * half + e, 16 + 16 * jj : 32 + 16 * jj, lanes] = t.astype(jnp.bfloat16)
            return 0

        lax.fori_loop(0, 24, step, 0)

    def norm_rows(g, r, own_row=None):
        v = T[g, pl.ds(r, 16), :].astype(jnp.float32)
        mean = jnp.sum(v, axis=1, keepdims=True) * (1.0 / 6144)
        d = v - mean
        var = jnp.sum(d * d, axis=1, keepdims=True) * (1.0 / 6144)
        n = (d * lax.rsqrt(var + 1e-06) * gain[...]).astype(jnp.bfloat16)
        at = pl.multiple_of(g * 64 + r, 16)
        for j in range(GROUPS):
            N[j, pl.ds(at, 16), :] = n[:, j * HD : (j + 1) * HD]
            if own_row is not None:
                NO[j, pl.ds(own_row, 16), :] = n[:, j * HD : (j + 1) * HD]

    def norm_own():
        def step(i, _):
            g, half = i // 2, i % 2
            norm_rows(1 + g, pl.multiple_of(16 + 16 * half, 16), pl.multiple_of(16 * i, 16))
            return 0

        lax.fori_loop(0, 8, step, 0)

    def norm_vertical():
        def step(i, _):
            norm_rows(1 + i // 2, pl.multiple_of(48 * (i % 2), 16))
            return 0

        lax.fori_loop(0, 8, step, 0)

    def norm_sides():
        def step(i, _):
            norm_rows(5 * (i // 4), pl.multiple_of(16 * (i % 4), 16))
            return 0

        lax.fori_loop(0, 8, step, 0)

    def rows_of(ref, cb, part):
        cols = []
        for j in range(KEEP):
            i = QI[j, cb]
            if part == "sides":
                cols.append(jnp.concatenate([ref[i, 0:64, :], ref[i, 320:384, :]], axis=0))
            elif part in ("middle", "both"):
                cols.append(ref[i, 64:320, :])
            else:
                cols.append(ref[i])
        return jnp.concatenate(cols, axis=1)

    def project(ref, cb, part):
        w = W[pl.ds(cb * KEEP, KEEP)].reshape(KEEP * HD, HD)
        return jnp.dot(rows_of(ref, cb, part), w, preferred_element_type=jnp.float32).astype(jnp.bfloat16)

    def chunk(lo, count, part):
        @pl.when(lo < HEADS)
        def _():
            if part in ("own", "both", "all"):
                for e in range(count):
                    Q[lo + e] = project(NO, lo + e, "own")

        @pl.when(lo >= HEADS)
        def _():
            if part == "own":
                return
            for e in range(count):
                r = project(N, lo + e, part)
                if part in ("middle", "both"):
                    KV[lo + e - HEADS, 64:320, :] = r
                elif part == "sides":
                    KV[lo + e - HEADS, 0:64, :] = r[0:64]
                    KV[lo + e - HEADS, 320:384, :] = r[64:128]
                else:
                    KV[lo + e - HEADS] = r

    def shard(f, part):
        def step(c, _):
            chunk(f * SHARD + c * 3, 3, part)
            return 0

        lax.fori_loop(0, SHARD // 3, step, 0)

    def make_shifted():
        SHIFT[0] = jnp.zeros((HEADS, HD), jnp.float32)
        SHIFT[0, :, 0:81] = rel[...]
        v = SHIFT[0]
        lane = lax.broadcasted_iota(jnp.int32, (HEADS, HD), 1)
        rows = [jnp.zeros_like(v)] * 3
        for a in range(9):
            for e in range(3):
                at = (lane + (3 if e == 2 else 0)) % HD
                moved = pltpu.roll(v, (-5 * a - 4 * e) % HD, 1)
                rows[e] = jnp.where((at >= 4 * a) & (at < 4 * a + 4), moved, rows[e])
        SHIFT[0] = rows[0]
        SHIFT[1] = pltpu.roll(rows[0], HD - 4, 1)
        SHIFT[2] = rows[1]
        SHIFT[3] = rows[2]

    def make_bias():
        make_shifted()
        lane = lax.broadcasted_iota(jnp.int32, (8, PAIR), 1)
        sub = lax.broadcasted_iota(jnp.int32, (8, PAIR), 0)
        ky, kx = (lane % 64) // 4 - 4, (lane // 64) * 4 + lane % 4 - 4
        inside = (ky + row * TH >= 0) & (ky + row * TH < 8 * TH)
        low = lax.broadcasted_iota(jnp.int32, (8, HD), 1) < 64
        right = lax.broadcasted_iota(jnp.int32, (8, HD), 1) % 4 >= lax.broadcasted_iota(jnp.int32, (8, HD), 0) % 4
        for i in range(4):
            qy, qx = 2 * i + sub // 4, sub % 4
            ok = inside & (jnp.abs(ky - qy) <= RADIUS) & (jnp.abs(kx - qx) <= RADIUS)

            def step(h, _):
                r = [
                    pltpu.roll(jnp.broadcast_to(SHIFT[e, pl.ds(h, 1), :], (8, HD)), 8 * i, 1, stride=1, stride_axis=0) for e in range(4)
                ]
                same = jnp.where(right, r[2], r[1])
                first = jnp.where(ok[:, :HD], jnp.where(low, r[0], pltpu.roll(same, 64, 1)), NEG)
                last = jnp.where(ok[:, HD:], r[3], NEG)
                turned = pltpu.roll(first, 64, 1)
                B[h, 8 * i : 8 * i + 8, :] = jnp.concatenate([first, jnp.where(low, last, NEG)], axis=1)
                B[h, 32 + 8 * i : 40 + 8 * i, :] = jnp.concatenate([jnp.where(low, NEG, turned), jnp.where(low, turned, pltpu.roll(last, 64, 1))], axis=1)
                return 0

            lax.fori_loop(0, HEADS, step, 0, unroll=4)
        wide = lax.broadcasted_iota(jnp.int32, (8, PAIR), 1)
        EDGE[0] = jnp.where((wide < 64) & (col == 0), NEG, 0.0)
        EDGE[1] = jnp.where((wide >= 192) & (col == 7), NEG, 0.0)

    def attend(h0, count):
        pairs = [(h0 + i, p) for i in range(count) for p in range(2)]
        ss_, ws_, os_ = [], [], []
        for h, p in pairs:
            ss_.append(lax.dot_general(
                Q[h, 64 * p : 64 * p + 64, :], KV[h, 128 * p : 128 * p + PAIR, :], (((1,), (1,)), ((), ())), preferred_element_type=jnp.float32
            ))
        for (h, p), s in zip(pairs, ss_):
            s = s * (HD ** -0.5) + B[h] + EDGE[p, 0:1, :]
            w = jnp.exp(s - jnp.max(s, axis=1, keepdims=True))
            ws_.append((w.astype(jnp.bfloat16), jnp.sum(w, axis=1, keepdims=True)))
        for (h, p), (w, total) in zip(pairs, ws_):
            o = jnp.dot(w, KV[HEADS + h, 128 * p : 128 * p + PAIR, :], preferred_element_type=jnp.float32) / total
            os_.append((o[0:32], o[32:64]))
        for i in range(count):
            outs = os_[2 * i] + os_[2 * i + 1]
            for j in range(4):
                halves = []
                for half in range(2):
                    halves.append(swap_fours(outs[2 * half][8 * j : 8 * j + 8], outs[2 * half + 1][8 * j : 8 * j + 8]))
                for e in range(2):
                    both = jnp.concatenate([halves[0][e], halves[1][e]], axis=0)
                    ATT[h0 + i, 32 * j + 16 * e : 32 * j + 16 * e + 16, :] = both.astype(jnp.bfloat16)

    def output(cb):
        lhs = jnp.concatenate([ATT[OI[j, cb]] for j in range(KEEP_O)], axis=1)
        w = WO[pl.ds(cb * KEEP_O, KEEP_O)].reshape(KEEP_O * HD, HD)
        acc = jnp.dot(lhs, w, preferred_element_type=jnp.float32)
        lanes = pl.ds(pl.multiple_of(cb * HD, HD), HD)
        out[:, lanes] = (acc + NAT[:, lanes].astype(jnp.float32)).astype(jnp.bfloat16)

    c_tok.wait()
    regroup()
    h_start("NR", "SR", "N", "S", "ND", "SD", "W", "E")

    @pl.when(jnp.logical_not(up))
    def _():
        T[0:3, 0:16, :] = jnp.zeros((3, 16, 6144), jnp.bfloat16)
        T[5, 0:16, :] = jnp.zeros((16, 6144), jnp.bfloat16)

    @pl.when(jnp.logical_not(down))
    def _():
        T[0:3, 48:64, :] = jnp.zeros((3, 16, 6144), jnp.bfloat16)
        T[5, 48:64, :] = jnp.zeros((16, 6144), jnp.bfloat16)

    @pl.when(jnp.logical_not(west))
    def _():
        T[0] = jnp.zeros((64, 6144), jnp.bfloat16)

    @pl.when(jnp.logical_not(east))
    def _():
        T[5] = jnp.zeros((64, 6144), jnp.bfloat16)

    def pump_x(i):
        for j in (i, 4 + i):
            a_recv(j).wait_recv()
            a_forward(j).start()
            s_send(j).start()

    def pump(*items):
        for j in items:
            a_recv(j).wait_recv()
            s_send(j).start()

    norm_own()
    pump_x(0)
    make_bias()
    pump_x(1)
    c_wq.wait()
    c_qi.wait()
    shard(f_own, "own")
    pump_x(2)
    h_wait("NR", "SR")
    h_start("NF", "SF")
    o_starts = [o_first(0), o_first(1)]
    for c in o_starts:
        c.start()
    sb_send.start()
    sa_recv.wait_recv()
    shard(f_sib, "own")
    pump_x(3)
    h_wait("N", "S", "ND", "SD", "NF", "SF")
    h_start("NW", "NE", "SW", "SE")
    norm_vertical()
    pump(8, 9, 10, 14)
    for j in range(2):
        o_recv(j).wait_recv()
        o_forward(j).start()
        os_send(j).start()
    shard(f_own, "middle")
    pump(11, 15, 12, 16)
    shard(f_sib, "middle")
    pump(13, 17)

    def received(j, part):
        chunk(f_oth * SHARD + came[j], 2, part)
        for i in range(2):
            s_recv(j + i).wait_recv()
        chunk(f_osb * SHARD + came[j], 2, part)

    for j in (0, 4, 2, 6, 8):
        received(j, "both")
    h_wait("W", "E", "NW", "NE", "SW", "SE")
    norm_sides()
    shard(f_own, "sides")
    shard(f_sib, "sides")
    for j in (0, 4, 2, 6, 8):
        chunk(f_oth * SHARD + came[j], 2, "sides")
        chunk(f_osb * SHARD + came[j], 2, "sides")
    for j in (10, 14, 12, 16):
        received(j, "all")

    def head(i, _):
        attend(3 * i, 3)
        return 0

    lax.fori_loop(0, HEADS // 3, head, 0)

    for j in range(2, 4):
        o_recv(j).wait_recv()
        os_send(j).start()
    c_wo.wait()
    c_oi.wait()
    sb_recv.wait_recv()
    for j in range(4):
        os_recv(j).wait_recv()

    def column(cb, _):
        output(cb)
        return 0

    lax.fori_loop(0, GROUPS, column, 0, unroll=4)

    for c in a_starts + o_starts + [sa_send, sb_send]:
        c.wait_send()
    for j in range(8):
        a_forward(j).wait_send()
    for j in range(2):
        o_forward(j).wait_send()
    for j in range(18):
        s_send(j).wait_send()
    for j in range(4):
        os_send(j).wait_send()
    h_wait_send(*names)


def body(tokens, ln_gain, qkv_blocks, qkv_index, out_blocks, out_index, rel_bias):
    any_, vmem = pl.BlockSpec(memory_space=pl.ANY), pl.BlockSpec(memory_space=pltpu.VMEM)
    dma = lambda n: pltpu.SemaphoreType.DMA((n,))
    bf = jnp.bfloat16
    mixed = pl.pallas_call(
        kernel,
        out_shape=jax.ShapeDtypeStruct((OWN, 6144), bf),
        in_specs=[any_, any_, any_, vmem, vmem, any_, any_],
        out_specs=vmem,
        scratch_shapes=[
            pltpu.VMEM((OWN, 6144), bf),
            pltpu.VMEM((6, 64, 6144), bf),
            pltpu.VMEM((GROUPS, ALL, HD), bf),
            pltpu.VMEM((GROUPS, OWN, HD), bf),
            pltpu.VMEM((432, HD, HD), bf),
            pltpu.VMEM((144, HD, HD), bf),
            pltpu.VMEM((HEADS, OWN, HD), bf),
            pltpu.VMEM((2 * HEADS, ALL, HD), bf),
            pltpu.VMEM((HEADS, OWN, HD), bf),
            pltpu.VMEM((HEADS, 64, PAIR), jnp.float32),
            pltpu.VMEM((2, 8, PAIR), jnp.float32),
            pltpu.VMEM((4, HEADS, HD), jnp.float32),
            pltpu.SMEM((KEEP, 3 * HEADS), jnp.int32),
            pltpu.SMEM((KEEP_O, GROUPS), jnp.int32),
            dma(5), dma(14), dma(14), dma(18), dma(18), dma(18), dma(18), dma(4), dma(4), dma(4), dma(4), dma(2), dma(2),
        ],
        compiler_params=pltpu.CompilerParams(collective_id=0, has_side_effects=True, vmem_limit_bytes=58 * 2**20),
        cost_estimate=pl.CostEstimate(flops=6 * 10**9, bytes_accessed=30 * 2**20, transcendentals=10**6),
        name="block",
    )(
        qkv_index.T, out_index.T, tokens.reshape(OWN, -1), ln_gain.reshape(1, -1), rel_bias,
        qkv_blocks.reshape(SHARD * KEEP, HD, HD), out_blocks.reshape(SHARD_O * KEEP_O, HD, HD),
    )
    return mixed.reshape(1, TH, TW, -1)


def solution(mesh):
    in_specs = (
        P("fsdp", "row", "col", None),
        P(),
        P("fsdp", None, None, None),
        P(),
        P("fsdp", None, None, None),
        P(),
        P(),
    )
    out_specs = P("fsdp", "row", "col", None)
    return jax.shard_map(body, mesh=mesh, in_specs=in_specs, out_specs=out_specs, check_vma=False)
```

```python
import jax
import jax.numpy as jnp
from jax import lax
from jax.experimental import pallas as pl
from jax.experimental.pallas import tpu as pltpu
from jax.sharding import PartitionSpec as P

MESH = pl.DeviceIdType.MESH
HD = 128
HEADS = 24
KEEP = 6
KEEP_O = 3
RADIUS = 4
TH, TW = 8, 16
OWN = TH * TW
ALL = (TH + 2 * RADIUS) * (TW + 2 * RADIUS)
PAIR = 256
GROUPS = 48
SHARD = 18
SHARD_O = 12
NEG = -1e30
VERT = ((64, 16), (112, 32), (176, 32), (240, 32), (304, 16))


def kernel(
    qi_any, oi_any, tok, gain, rel, wq, wo, out,
    NAT, T, N, NO, W, WO, Q, KV, ATT, B, EDGE, SHIFT, QI, OI,
    loc, hs, hr, ws, wr, ss, sr, bs, br, bss, bsr, os, orr,
):
    row, col, fs_ = lax.axis_index("row"), lax.axis_index("col"), lax.axis_index("fsdp")
    x, y, z, k = (row // 4) * 2 + fs_ // 2, row % 4, col, fs_ % 2

    def dev(dx, dy, dz, dk):
        xx, yy, zz, kk = (x + dx) % 4, (y + dy) % 4, (z + dz) % 8, (k + dk) % 2
        return ((xx // 2) * 4 + yy, zz, (xx % 2) * 2 + kk)

    def tile(dr, dc):
        return ((row + dr + 8) % 8, (col + dc + 8) % 8, fs_)

    f_own = fs_
    f_sib = (x % 2) * 2 + (1 - k)
    f_oth = (1 - x % 2) * 2 + k
    f_osb = (1 - x % 2) * 2 + (1 - k)
    cz, cy = z % 2, y % 2
    sib = dev(0, 0, 0, 1)
    xp, xm = dev(1, 0, 0, 0), dev(3, 0, 0, 0)
    yp, ym = dev(0, 1, 0, 0), dev(0, 3, 0, 0)
    zp, zm = dev(0, 0, 1, 0), dev(0, 0, 7, 0)
    ya, yb, za, zb = 4 * cy, 4 * (1 - cy), 8 + 4 * cz, 8 + 4 * (1 - cz)
    came = [ya + i for i in range(4)] + [za + i for i in range(4)] + [16 + cz, 17 - cz] + [yb + i for i in range(4)] + [zb + i for i in range(4)]

    c_qi = pltpu.make_async_copy(qi_any, QI, loc.at[3])
    c_oi = pltpu.make_async_copy(oi_any, OI, loc.at[4])
    c_qi.start()
    c_oi.start()
    c_tok = pltpu.make_async_copy(tok, NAT, loc.at[0])
    c_wq = pltpu.make_async_copy(wq, W.at[pl.ds(f_own * 108, 108)], loc.at[1])
    c_wo = pltpu.make_async_copy(wo, WO.at[pl.ds(f_own * 36, 36)], loc.at[2])
    c_tok.start()
    c_wq.start()
    c_wo.start()

    partners = [sib, xp, xm, yp, ym, zp, zm, tile(1, 0), tile(-1, 0), dev(2, 0, 0, 0)]
    barrier = pltpu.get_barrier_semaphore()
    for p in partners:
        pl.semaphore_signal(barrier, inc=1, device_id=p, device_id_type=MESH)
    pl.semaphore_wait(barrier, len(partners))

    def rc(src, dst, s, r, to):
        return pltpu.make_async_remote_copy(src_ref=src, dst_ref=dst, send_sem=s, recv_sem=r, device_id=to, device_id_type=MESH)

    def a_ref(f, j):
        return W.at[pl.ds((f * SHARD + came[j]) * KEEP, KEEP)]

    def a_first(j):
        src = wq.at[pl.ds(came[j] * KEEP, KEEP)]
        return rc(src, a_ref(f_own, j), ws.at[j], wr.at[j], xp if j < 4 or j == 8 else xm)

    def a_forward(j):
        d = a_ref(f_oth, j)
        to = zm if j == 8 else (yp, ym, zp, zm)[(j // 4) * 2 + j % 2]
        at = 9 if j == 8 else 10 + j
        return rc(d, d, ws.at[at], wr.at[at], to)

    def a_recv(j):
        d = a_ref(f_oth, j)
        return rc(d, d, ws.at[j], wr.at[j], sib)

    def s_send(j):
        d = a_ref(f_oth, j)
        return rc(d, d, ss.at[j], sr.at[j], sib)

    def s_recv(j):
        d = a_ref(f_osb, j)
        return rc(d, d, ss.at[j], sr.at[j], sib)

    parts = [6 * cy, 12 + 12 * cz, 6 * (1 - cy), 12 + 12 * (1 - cz)]
    sizes = (6, 12, 6, 12)

    def o_ref(f, j):
        return WO.at[pl.ds(f * 36 + parts[j], sizes[j])]

    def o_first(j):
        return rc(wo.at[pl.ds(parts[j], sizes[j])], o_ref(f_own, j), bs.at[j], br.at[j], (xp, xm)[j])

    def o_forward(j):
        d = o_ref(f_oth, j)
        return rc(d, d, bs.at[2 + j], br.at[2 + j], (yp, zp)[j])

    def o_recv(j):
        d = o_ref(f_oth, j)
        return rc(d, d, bs.at[j], br.at[j], sib)

    def os_send(j):
        d = o_ref(f_oth, j)
        return rc(d, d, bss.at[j], bsr.at[j], sib)

    def os_recv(j):
        d = o_ref(f_osb, j)
        return rc(d, d, bss.at[j], bsr.at[j], sib)

    sa_send = rc(wq, W.at[pl.ds(f_own * 108, 108)], os.at[0], orr.at[0], sib)
    d_sa = W.at[pl.ds(f_sib * 108, 108)]
    sa_recv = rc(d_sa, d_sa, os.at[0], orr.at[0], sib)
    sb_send = rc(wo, WO.at[pl.ds(f_own * 36, 36)], os.at[1], orr.at[1], sib)
    d_sb = WO.at[pl.ds(f_sib * 36, 36)]
    sb_recv = rc(d_sb, d_sb, os.at[1], orr.at[1], sib)

    up, down, west, east = row > 0, row < 7, col > 0, col < 7
    four, low2, high2, across = pl.ds(1, 4), pl.ds(1, 2), pl.ds(3, 2), dev(2, 0, 0, 0)
    halo = dict(
        N=((four, pl.ds(32, 16)), (four, pl.ds(0, 16)), tile(1, 0), down & (row != 3), up & (row != 4)),
        S=((four, pl.ds(16, 16)), (four, pl.ds(48, 16)), tile(-1, 0), up & (row != 4), down & (row != 3)),
        W=((4, pl.ds(16, 32)), (0, pl.ds(16, 32)), tile(0, 1), east, west),
        E=((1, pl.ds(16, 32)), (5, pl.ds(16, 32)), tile(0, -1), west, east),
        NW=((4, pl.ds(0, 16)), (0, pl.ds(0, 16)), tile(0, 1), up & east, up & west),
        NE=((1, pl.ds(0, 16)), (5, pl.ds(0, 16)), tile(0, -1), up & west, up & east),
        SW=((4, pl.ds(48, 16)), (0, pl.ds(48, 16)), tile(0, 1), down & east, down & west),
        SE=((1, pl.ds(48, 16)), (5, pl.ds(48, 16)), tile(0, -1), down & west, down & east),
        ND=((low2, pl.ds(32, 16)), (low2, pl.ds(0, 16)), tile(1, 0), row == 3, row == 4),
        NR=((high2, pl.ds(32, 16)), (high2, pl.ds(0, 16)), yp, row == 3, row == 0),
        NF=((high2, pl.ds(0, 16)), (high2, pl.ds(0, 16)), across, row == 0, row == 4),
        SD=((low2, pl.ds(16, 16)), (low2, pl.ds(48, 16)), tile(-1, 0), row == 4, row == 3),
        SR=((high2, pl.ds(16, 16)), (high2, pl.ds(48, 16)), ym, row == 4, row == 7),
        SF=((high2, pl.ds(48, 16)), (high2, pl.ds(48, 16)), across, row == 7, row == 3),
    )
    names = tuple(halo)

    def h_copy(name):
        src, dst, to, _, _ = halo[name]
        j = names.index(name)
        return rc(T.at[src], T.at[dst], hs.at[j], hr.at[j], to)

    def h_start(*which):
        for name in which:
            @pl.when(halo[name][3])
            def _():
                h_copy(name).start()

    def h_wait_send(*which):
        for name in which:
            @pl.when(halo[name][3])
            def _():
                h_copy(name).wait_send()

    def h_wait(*which):
        for name in which:
            d = T.at[halo[name][1]]
            j = names.index(name)

            @pl.when(halo[name][4])
            def _():
                rc(d, d, hs.at[j], hr.at[j], sib).wait_recv()

    a_starts = [a_first(j) for j in (0, 4, 1, 5, 2, 6, 3, 7, 8)]
    for c in a_starts[:4]:
        c.start()
    sa_send.start()

    def swap_fours(a, b):
        low = lax.broadcasted_iota(jnp.int32, a.shape, 0) < 4
        return jnp.where(low, a, pltpu.roll(b, 4, 0)), jnp.where(low, pltpu.roll(a, 4, 0), b)

    def regroup():
        def step(i, _):
            lanes = pl.ds(pl.multiple_of(i * 256, 256), 256)
            for jj in range(2):
                v = NAT[pl.ds(64 * jj, 64), lanes].astype(jnp.float32)
                for half in range(2):
                    pairs = [swap_fours(v[32 * j + 8 * half : 32 * j + 8 * half + 8], v[32 * j + 16 + 8 * half : 32 * j + 24 + 8 * half]) for j in range(2)]
                    for e in range(2):
                        t = jnp.concatenate([pairs[0][e], pairs[1][e]], axis=0)
                        T[1 + 2 * half + e, 16 + 16 * jj : 32 + 16 * jj, lanes] = t.astype(jnp.bfloat16)
            return 0

        lax.fori_loop(0, 24, step, 0)

    def norm_rows(g, r, own_row=None):
        v = T[g, pl.ds(r, 16), :].astype(jnp.float32)
        mean = jnp.sum(v, axis=1, keepdims=True) * (1.0 / 6144)
        d = v - mean
        var = jnp.sum(d * d, axis=1, keepdims=True) * (1.0 / 6144)
        n = (d * lax.rsqrt(var + 1e-06) * gain[...]).astype(jnp.bfloat16)
        at = pl.multiple_of(g * 64 + r, 16)
        for j in range(GROUPS):
            N[j, pl.ds(at, 16), :] = n[:, j * HD : (j + 1) * HD]
            if own_row is not None:
                NO[j, pl.ds(own_row, 16), :] = n[:, j * HD : (j + 1) * HD]

    def norm_own():
        def step(i, _):
            g, half = i // 2, i % 2
            norm_rows(1 + g, pl.multiple_of(16 + 16 * half, 16), pl.multiple_of(16 * i, 16))
            return 0

        lax.fori_loop(0, 8, step, 0)

    def norm_vertical():
        def step(i, _):
            norm_rows(1 + i // 2, pl.multiple_of(48 * (i % 2), 16))
            return 0

        lax.fori_loop(0, 8, step, 0)

    def norm_sides():
        def step(i, _):
            norm_rows(5 * (i // 4), pl.multiple_of(16 * (i % 4), 16))
            return 0

        lax.fori_loop(0, 8, step, 0)

    def rows_of(ref, cb, part):
        cols = []
        for j in range(KEEP):
            i = QI[j, cb]
            if part == "sides":
                cols.append(jnp.concatenate([ref[i, 0:64, :], ref[i, 320:384, :]], axis=0))
            elif part == "vert":
                cols.append(jnp.concatenate([ref[i, a : a + n, :] for a, n in VERT], axis=0))
            else:
                cols.append(ref[i])
        return jnp.concatenate(cols, axis=1)

    def project(ref, cb, part):
        w = W[pl.ds(cb * KEEP, KEEP)].reshape(KEEP * HD, HD)
        return jnp.dot(rows_of(ref, cb, part), w, preferred_element_type=jnp.float32).astype(jnp.bfloat16)

    def chunk(lo, count, part):
        if part in ("own", "all"):
            @pl.when(lo < HEADS)
            def _():
                for e in range(count):
                    Q[lo + e] = project(NO, lo + e, "own")

        @pl.when(lo >= HEADS)
        def _():
            for e in range(count):
                at = lo + e - HEADS
                r = project(NO if part == "own" else N, lo + e, part)
                if part == "own":
                    for g in range(4):
                        KV[at, 64 * g + 80 : 64 * g + 112, :] = r[32 * g : 32 * g + 32]
                elif part == "vert":
                    k = 0
                    for a, n in VERT:
                        KV[at, a : a + n, :] = r[k : k + n]
                        k += n
                elif part == "sides":
                    KV[at, 0:64, :] = r[0:64]
                    KV[at, 320:384, :] = r[64:128]
                else:
                    KV[at] = r

    def shard(f, part):
        def step(c, _):
            chunk(f * SHARD + c * 3, 3, part)
            return 0

        lax.fori_loop(0, SHARD // 3, step, 0)

    def make_shifted():
        SHIFT[0] = jnp.zeros((HEADS, HD), jnp.float32)
        SHIFT[0, :, 0:81] = rel[...]
        v = SHIFT[0]
        lane = lax.broadcasted_iota(jnp.int32, (HEADS, HD), 1)
        rows = [jnp.zeros_like(v)] * 3
        for a in range(9):
            for e in range(3):
                at = (lane + (3 if e == 2 else 0)) % HD
                moved = pltpu.roll(v, (-5 * a - 4 * e) % HD, 1)
                rows[e] = jnp.where((at >= 4 * a) & (at < 4 * a + 4), moved, rows[e])
        SHIFT[0] = rows[0]
        SHIFT[1] = pltpu.roll(rows[0], HD - 4, 1)
        SHIFT[2] = rows[1]
        SHIFT[3] = rows[2]

    def make_bias():
        make_shifted()
        lane = lax.broadcasted_iota(jnp.int32, (8, PAIR), 1)
        sub = lax.broadcasted_iota(jnp.int32, (8, PAIR), 0)
        ky, kx = (lane % 64) // 4 - 4, (lane // 64) * 4 + lane % 4 - 4
        inside = (ky + row * TH >= 0) & (ky + row * TH < 8 * TH)
        low = lax.broadcasted_iota(jnp.int32, (8, HD), 1) < 64
        right = lax.broadcasted_iota(jnp.int32, (8, HD), 1) % 4 >= lax.broadcasted_iota(jnp.int32, (8, HD), 0) % 4
        for i in range(4):
            qy, qx = 2 * i + sub // 4, sub % 4
            ok = inside & (jnp.abs(ky - qy) <= RADIUS) & (jnp.abs(kx - qx) <= RADIUS)

            def step(h, _):
                r = [
                    pltpu.roll(jnp.broadcast_to(SHIFT[e, pl.ds(h, 1), :], (8, HD)), 8 * i, 1, stride=1, stride_axis=0) for e in range(4)
                ]
                same = jnp.where(right, r[2], r[1])
                first = jnp.where(ok[:, :HD], jnp.where(low, r[0], pltpu.roll(same, 64, 1)), NEG)
                last = jnp.where(ok[:, HD:], r[3], NEG)
                turned = pltpu.roll(first, 64, 1)
                B[h, 8 * i : 8 * i + 8, :] = jnp.concatenate([first, jnp.where(low, last, NEG)], axis=1)
                B[h, 32 + 8 * i : 40 + 8 * i, :] = jnp.concatenate([jnp.where(low, NEG, turned), jnp.where(low, turned, pltpu.roll(last, 64, 1))], axis=1)
                return 0

            lax.fori_loop(0, HEADS, step, 0, unroll=4)
        wide = lax.broadcasted_iota(jnp.int32, (8, PAIR), 1)
        EDGE[0] = jnp.where((wide < 64) & (col == 0), NEG, 0.0)
        EDGE[1] = jnp.where((wide >= 192) & (col == 7), NEG, 0.0)

    def attend(h0, count):
        pairs = [(h0 + i, p) for i in range(count) for p in range(2)]
        ss_, ws_, os_ = [], [], []
        for h, p in pairs:
            ss_.append(lax.dot_general(
                Q[h, 64 * p : 64 * p + 64, :], KV[h, 128 * p : 128 * p + PAIR, :], (((1,), (1,)), ((), ())), preferred_element_type=jnp.float32
            ))
        for (h, p), s in zip(pairs, ss_):
            s = s * (HD ** -0.5) + B[h] + EDGE[p, 0:1, :]
            w = jnp.exp(s - jnp.max(s, axis=1, keepdims=True))
            ws_.append((w.astype(jnp.bfloat16), jnp.sum(w, axis=1, keepdims=True)))
        for (h, p), (w, total) in zip(pairs, ws_):
            o = jnp.dot(w, KV[HEADS + h, 128 * p : 128 * p + PAIR, :], preferred_element_type=jnp.float32) / total
            os_.append((o[0:32], o[32:64]))
        for i in range(count):
            outs = os_[2 * i] + os_[2 * i + 1]
            for j in range(4):
                halves = []
                for half in range(2):
                    halves.append(swap_fours(outs[2 * half][8 * j : 8 * j + 8], outs[2 * half + 1][8 * j : 8 * j + 8]))
                for e in range(2):
                    both = jnp.concatenate([halves[0][e], halves[1][e]], axis=0)
                    ATT[h0 + i, 32 * j + 16 * e : 32 * j + 16 * e + 16, :] = both.astype(jnp.bfloat16)

    def output(cb):
        lhs = jnp.concatenate([ATT[OI[j, cb]] for j in range(KEEP_O)], axis=1)
        w = WO[pl.ds(cb * KEEP_O, KEEP_O)].reshape(KEEP_O * HD, HD)
        acc = jnp.dot(lhs, w, preferred_element_type=jnp.float32)
        lanes = pl.ds(pl.multiple_of(cb * HD, HD), HD)
        out[:, lanes] = (acc + NAT[:, lanes].astype(jnp.float32)).astype(jnp.bfloat16)

    c_tok.wait()
    regroup()
    h_start("NR", "SR", "N", "S", "ND", "SD", "W", "E")
    for c in a_starts[4:]:
        c.start()

    @pl.when(jnp.logical_not(up))
    def _():
        T[0:3, 0:16, :] = jnp.zeros((3, 16, 6144), jnp.bfloat16)
        T[5, 0:16, :] = jnp.zeros((16, 6144), jnp.bfloat16)

    @pl.when(jnp.logical_not(down))
    def _():
        T[0:3, 48:64, :] = jnp.zeros((3, 16, 6144), jnp.bfloat16)
        T[5, 48:64, :] = jnp.zeros((16, 6144), jnp.bfloat16)

    @pl.when(jnp.logical_not(west))
    def _():
        T[0] = jnp.zeros((64, 6144), jnp.bfloat16)

    @pl.when(jnp.logical_not(east))
    def _():
        T[5] = jnp.zeros((64, 6144), jnp.bfloat16)

    def pump_x(i):
        for j in (i, 4 + i):
            a_recv(j).wait_recv()
            a_forward(j).start()
            s_send(j).start()

    def pump(*items):
        for j in items:
            a_recv(j).wait_recv()
            s_send(j).start()

    norm_own()
    pump_x(0)
    make_bias()
    pump_x(1)
    h_wait("NR", "SR")
    h_start("NF", "SF")
    c_wq.wait()
    c_qi.wait()
    shard(f_own, "own")
    pump_x(2)
    o_starts = [o_first(0), o_first(1)]
    for c in o_starts:
        c.start()
    sb_send.start()
    sa_recv.wait_recv()
    shard(f_sib, "own")
    pump_x(3)
    def base(f, j):
        return f * SHARD + (16 if j == 8 else came[j])

    def received(j, part):
        chunk(base(f_oth, j), 2, part)
        for i in range(2):
            s_recv(j + i).wait_recv()
        chunk(base(f_osb, j), 2, part)

    for j in (0, 4, 2, 6):
        received(j, "own")
    h_wait("N", "S", "ND", "SD", "NF", "SF")
    h_start("NW", "NE", "SW", "SE")
    norm_vertical()
    a_recv(8).wait_recv()
    a_forward(8).start()
    s_send(8).start()
    pump(10, 14)
    shard(f_own, "vert")
    pump(11, 15, 12, 16)
    shard(f_sib, "vert")
    pump(13, 17, 9)
    for j in range(2):
        o_recv(j).wait_recv()
        o_forward(j).start()
        os_send(j).start()

    for j in (0, 4, 2, 6):
        chunk(base(f_oth, j), 2, "vert")
        chunk(base(f_osb, j), 2, "vert")
    h_wait("W", "E", "NW", "NE", "SW", "SE")
    norm_sides()
    shard(f_own, "sides")
    shard(f_sib, "sides")
    for j in (0, 4, 2, 6):
        chunk(base(f_oth, j), 2, "sides")
        chunk(base(f_osb, j), 2, "sides")
    for j in (8, 10, 14, 12, 16):
        received(j, "all")

    def head(i, _):
        attend(3 * i, 3)
        return 0

    lax.fori_loop(0, HEADS // 6, head, 0)
    for j in range(2, 4):
        o_recv(j).wait_recv()
        os_send(j).start()
    lax.fori_loop(HEADS // 6, HEADS // 3, head, 0)
    c_wo.wait()
    c_oi.wait()
    sb_recv.wait_recv()
    for j in range(4):
        os_recv(j).wait_recv()

    def column(cb, _):
        output(cb)
        return 0

    lax.fori_loop(0, GROUPS, column, 0, unroll=4)

    for c in a_starts + o_starts + [sa_send, sb_send]:
        c.wait_send()
    for j in range(9):
        a_forward(j).wait_send()
    for j in range(2):
        o_forward(j).wait_send()
    for j in range(18):
        s_send(j).wait_send()
    for j in range(4):
        os_send(j).wait_send()
    h_wait_send(*names)


def body(tokens, ln_gain, qkv_blocks, qkv_index, out_blocks, out_index, rel_bias):
    any_, vmem = pl.BlockSpec(memory_space=pl.ANY), pl.BlockSpec(memory_space=pltpu.VMEM)
    dma = lambda n: pltpu.SemaphoreType.DMA((n,))
    bf = jnp.bfloat16
    mixed = pl.pallas_call(
        kernel,
        out_shape=jax.ShapeDtypeStruct((OWN, 6144), bf),
        in_specs=[any_, any_, any_, vmem, vmem, any_, any_],
        out_specs=vmem,
        scratch_shapes=[
            pltpu.VMEM((OWN, 6144), bf),
            pltpu.VMEM((6, 64, 6144), bf),
            pltpu.VMEM((GROUPS, ALL, HD), bf),
            pltpu.VMEM((GROUPS, OWN, HD), bf),
            pltpu.VMEM((432, HD, HD), bf),
            pltpu.VMEM((144, HD, HD), bf),
            pltpu.VMEM((HEADS, OWN, HD), bf),
            pltpu.VMEM((2 * HEADS, ALL, HD), bf),
            pltpu.VMEM((HEADS, OWN, HD), bf),
            pltpu.VMEM((HEADS, 64, PAIR), jnp.float32),
            pltpu.VMEM((2, 8, PAIR), jnp.float32),
            pltpu.VMEM((4, HEADS, HD), jnp.float32),
            pltpu.SMEM((KEEP, 3 * HEADS), jnp.int32),
            pltpu.SMEM((KEEP_O, GROUPS), jnp.int32),
            dma(5), dma(14), dma(14), dma(18), dma(18), dma(18), dma(18), dma(4), dma(4), dma(4), dma(4), dma(2), dma(2),
        ],
        compiler_params=pltpu.CompilerParams(collective_id=0, has_side_effects=True, vmem_limit_bytes=58 * 2**20),
        cost_estimate=pl.CostEstimate(flops=6 * 10**9, bytes_accessed=30 * 2**20, transcendentals=10**6),
        name="block",
    )(
        qkv_index.T, out_index.T, tokens.reshape(OWN, -1), ln_gain.reshape(1, -1), rel_bias,
        qkv_blocks.reshape(SHARD * KEEP, HD, HD), out_blocks.reshape(SHARD_O * KEEP_O, HD, HD),
    )
    return mixed.reshape(1, TH, TW, -1)


def solution(mesh):
    in_specs = (
        P("fsdp", "row", "col", None),
        P(),
        P("fsdp", None, None, None),
        P(),
        P("fsdp", None, None, None),
        P(),
        P(),
    )
    out_specs = P("fsdp", "row", "col", None)
    return jax.shard_map(body, mesh=mesh, in_specs=in_specs, out_specs=out_specs, check_vma=False)
```

```python
import jax
import jax.numpy as jnp
from jax import lax
from jax.experimental import pallas as pl
from jax.experimental.pallas import tpu as pltpu
from jax.sharding import PartitionSpec as P

MESH = pl.DeviceIdType.MESH
HD = 128
HEADS = 24
KEEP = 6
KEEP_O = 3
RADIUS = 4
TH, TW = 8, 16
OWN = TH * TW
ALL = (TH + 2 * RADIUS) * (TW + 2 * RADIUS)
PAIR = 256
GROUPS = 48
SHARD = 18
SHARD_O = 12
NEG = -1e30
CORNERS = (0, 48, 320, 368)
VERT = ((64, 16), (112, 32), (176, 32), (240, 32), (304, 16))


def kernel(
    qi_any, oi_any, tok, gain, rel, wq, wo, out,
    NAT, T, N, NO, W, WO, Q, KV, ATT, B, EDGE, SHIFT, QI, OI,
    loc, hs, hr, ws, wr, ss, sr, bs, br, bss, bsr, os, orr,
):
    row, col, fs_ = lax.axis_index("row"), lax.axis_index("col"), lax.axis_index("fsdp")
    x, y, z, k = (row // 4) * 2 + fs_ // 2, row % 4, col, fs_ % 2

    def dev(dx, dy, dz, dk):
        xx, yy, zz, kk = (x + dx) % 4, (y + dy) % 4, (z + dz) % 8, (k + dk) % 2
        return ((xx // 2) * 4 + yy, zz, (xx % 2) * 2 + kk)

    def tile(dr, dc):
        return ((row + dr + 8) % 8, (col + dc + 8) % 8, fs_)

    f_own = fs_
    f_sib = (x % 2) * 2 + (1 - k)
    f_oth = (1 - x % 2) * 2 + k
    f_osb = (1 - x % 2) * 2 + (1 - k)
    cz, cy = z % 2, y % 2
    sib = dev(0, 0, 0, 1)
    xp, xm = dev(1, 0, 0, 0), dev(3, 0, 0, 0)
    yp, ym = dev(0, 1, 0, 0), dev(0, 3, 0, 0)
    zp, zm = dev(0, 0, 1, 0), dev(0, 0, 7, 0)
    ya, yb, za, zb = 4 * cy, 4 * (1 - cy), 8 + 4 * cz, 8 + 4 * (1 - cz)
    came = [ya + i for i in range(4)] + [za + i for i in range(4)] + [16 + cz, 17 - cz] + [yb + i for i in range(4)] + [zb + i for i in range(4)]

    c_qi = pltpu.make_async_copy(qi_any, QI, loc.at[3])
    c_oi = pltpu.make_async_copy(oi_any, OI, loc.at[4])
    c_qi.start()
    c_oi.start()
    c_tok = pltpu.make_async_copy(tok, NAT, loc.at[0])
    c_wq = pltpu.make_async_copy(wq, W.at[pl.ds(f_own * 108, 108)], loc.at[1])
    c_wo = pltpu.make_async_copy(wo, WO.at[pl.ds(f_own * 36, 36)], loc.at[2])
    c_tok.start()
    c_wq.start()
    c_wo.start()

    partners = [sib, xp, xm, yp, ym, zp, zm, tile(1, 0), tile(-1, 0), dev(2, 0, 0, 0)]
    barrier = pltpu.get_barrier_semaphore()
    for p in partners:
        pl.semaphore_signal(barrier, inc=1, device_id=p, device_id_type=MESH)
    pl.semaphore_wait(barrier, len(partners))

    def rc(src, dst, s, r, to):
        return pltpu.make_async_remote_copy(src_ref=src, dst_ref=dst, send_sem=s, recv_sem=r, device_id=to, device_id_type=MESH)

    def a_ref(f, j):
        return W.at[pl.ds((f * SHARD + came[j]) * KEEP, KEEP)]

    def a_first(j):
        src = wq.at[pl.ds(came[j] * KEEP, KEEP)]
        return rc(src, a_ref(f_own, j), ws.at[j], wr.at[j], xp if j < 4 or j == 8 else xm)

    def a_forward(j):
        d = a_ref(f_oth, j)
        to = zm if j == 8 else (yp, ym, zp, zm)[(j // 4) * 2 + j % 2]
        at = 9 if j == 8 else 10 + j
        return rc(d, d, ws.at[at], wr.at[at], to)

    def a_recv(j):
        d = a_ref(f_oth, j)
        return rc(d, d, ws.at[j], wr.at[j], sib)

    def s_send(j):
        d = a_ref(f_oth, j)
        return rc(d, d, ss.at[j], sr.at[j], sib)

    def s_recv(j):
        d = a_ref(f_osb, j)
        return rc(d, d, ss.at[j], sr.at[j], sib)

    parts = [6 * cy, 12 + 12 * cz, 6 * (1 - cy), 12 + 12 * (1 - cz)]
    sizes = (6, 12, 6, 12)

    def o_ref(f, j):
        return WO.at[pl.ds(f * 36 + parts[j], sizes[j])]

    def o_first(j):
        return rc(wo.at[pl.ds(parts[j], sizes[j])], o_ref(f_own, j), bs.at[j], br.at[j], (xp, xm)[j])

    def o_forward(j):
        d = o_ref(f_oth, j)
        return rc(d, d, bs.at[2 + j], br.at[2 + j], (yp, zp)[j])

    def o_recv(j):
        d = o_ref(f_oth, j)
        return rc(d, d, bs.at[j], br.at[j], sib)

    def os_send(j):
        d = o_ref(f_oth, j)
        return rc(d, d, bss.at[j], bsr.at[j], sib)

    def os_recv(j):
        d = o_ref(f_osb, j)
        return rc(d, d, bss.at[j], bsr.at[j], sib)

    sa_send = rc(wq, W.at[pl.ds(f_own * 108, 108)], os.at[0], orr.at[0], sib)
    d_sa = W.at[pl.ds(f_sib * 108, 108)]
    sa_recv = rc(d_sa, d_sa, os.at[0], orr.at[0], sib)
    sb_send = rc(wo, WO.at[pl.ds(f_own * 36, 36)], os.at[1], orr.at[1], sib)
    d_sb = WO.at[pl.ds(f_sib * 36, 36)]
    sb_recv = rc(d_sb, d_sb, os.at[1], orr.at[1], sib)

    up, down, west, east = row > 0, row < 7, col > 0, col < 7
    four, low2, high2, across = pl.ds(1, 4), pl.ds(1, 2), pl.ds(3, 2), dev(2, 0, 0, 0)
    halo = dict(
        N=((four, pl.ds(32, 16)), (four, pl.ds(0, 16)), tile(1, 0), down & (row != 3), up & (row != 4)),
        S=((four, pl.ds(16, 16)), (four, pl.ds(48, 16)), tile(-1, 0), up & (row != 4), down & (row != 3)),
        W=((4, pl.ds(16, 32)), (0, pl.ds(16, 32)), tile(0, 1), east, west),
        E=((1, pl.ds(16, 32)), (5, pl.ds(16, 32)), tile(0, -1), west, east),
        NW=((4, pl.ds(0, 16)), (0, pl.ds(0, 16)), tile(0, 1), up & east, up & west),
        NE=((1, pl.ds(0, 16)), (5, pl.ds(0, 16)), tile(0, -1), up & west, up & east),
        SW=((4, pl.ds(48, 16)), (0, pl.ds(48, 16)), tile(0, 1), down & east, down & west),
        SE=((1, pl.ds(48, 16)), (5, pl.ds(48, 16)), tile(0, -1), down & west, down & east),
        ND=((low2, pl.ds(32, 16)), (low2, pl.ds(0, 16)), tile(1, 0), row == 3, row == 4),
        NR=((high2, pl.ds(32, 16)), (high2, pl.ds(0, 16)), yp, row == 3, row == 0),
        NF=((high2, pl.ds(0, 16)), (high2, pl.ds(0, 16)), across, row == 0, row == 4),
        SD=((low2, pl.ds(16, 16)), (low2, pl.ds(48, 16)), tile(-1, 0), row == 4, row == 3),
        SR=((high2, pl.ds(16, 16)), (high2, pl.ds(48, 16)), ym, row == 4, row == 7),
        SF=((high2, pl.ds(48, 16)), (high2, pl.ds(48, 16)), across, row == 7, row == 3),
    )
    names = tuple(halo)

    def h_copy(name):
        src, dst, to, _, _ = halo[name]
        j = names.index(name)
        return rc(T.at[src], T.at[dst], hs.at[j], hr.at[j], to)

    def h_start(*which):
        for name in which:
            @pl.when(halo[name][3])
            def _():
                h_copy(name).start()

    def h_wait_send(*which):
        for name in which:
            @pl.when(halo[name][3])
            def _():
                h_copy(name).wait_send()

    def h_wait(*which):
        for name in which:
            d = T.at[halo[name][1]]
            j = names.index(name)

            @pl.when(halo[name][4])
            def _():
                rc(d, d, hs.at[j], hr.at[j], sib).wait_recv()

    a_starts = [a_first(j) for j in (0, 4, 1, 5, 2, 6, 3, 7, 8)]
    for c in a_starts[:4]:
        c.start()
    sa_send.start()

    def swap_fours(a, b):
        low = lax.broadcasted_iota(jnp.int32, a.shape, 0) < 4
        return jnp.where(low, a, pltpu.roll(b, 4, 0)), jnp.where(low, pltpu.roll(a, 4, 0), b)

    def regroup():
        def step(i, _):
            lanes = pl.ds(pl.multiple_of(i * 256, 256), 256)
            for jj in range(2):
                v = NAT[pl.ds(64 * jj, 64), lanes].astype(jnp.float32)
                for half in range(2):
                    pairs = [swap_fours(v[32 * j + 8 * half : 32 * j + 8 * half + 8], v[32 * j + 16 + 8 * half : 32 * j + 24 + 8 * half]) for j in range(2)]
                    for e in range(2):
                        t = jnp.concatenate([pairs[0][e], pairs[1][e]], axis=0)
                        T[1 + 2 * half + e, 16 + 16 * jj : 32 + 16 * jj, lanes] = t.astype(jnp.bfloat16)
            return 0

        lax.fori_loop(0, 24, step, 0)

    def norm_rows(g, r, own_row=None):
        v = T[g, pl.ds(r, 16), :].astype(jnp.float32)
        mean = jnp.sum(v, axis=1, keepdims=True) * (1.0 / 6144)
        d = v - mean
        var = jnp.sum(d * d, axis=1, keepdims=True) * (1.0 / 6144)
        n = (d * lax.rsqrt(var + 1e-06) * gain[...]).astype(jnp.bfloat16)
        at = pl.multiple_of(g * 64 + r, 16)
        for j in range(GROUPS):
            N[j, pl.ds(at, 16), :] = n[:, j * HD : (j + 1) * HD]
            if own_row is not None:
                NO[j, pl.ds(own_row, 16), :] = n[:, j * HD : (j + 1) * HD]

    def norm_own():
        def step(i, _):
            g, half = i // 2, i % 2
            norm_rows(1 + g, pl.multiple_of(16 + 16 * half, 16), pl.multiple_of(16 * i, 16))
            return 0

        lax.fori_loop(0, 8, step, 0)

    def norm_vertical():
        def step(i, _):
            norm_rows(1 + i // 2, pl.multiple_of(48 * (i % 2), 16))
            return 0

        lax.fori_loop(0, 8, step, 0)

    def norm_edges():
        def step(i, _):
            norm_rows(5 * (i // 2), pl.multiple_of(16 + 16 * (i % 2), 16), pl.multiple_of(OWN + 16 * i, 16))
            return 0

        lax.fori_loop(0, 4, step, 0)

    def norm_corners():
        def step(i, _):
            norm_rows(5 * (i // 2), pl.multiple_of(48 * (i % 2), 16))
            return 0

        lax.fori_loop(0, 4, step, 0)

    def rows_of(ref, cb, part):
        cols = []
        for j in range(KEEP):
            i = QI[j, cb]
            if part == "q":
                cols.append(ref[i, 0:OWN, :])
            elif part == "corners":
                cols.append(jnp.concatenate([ref[i, a : a + 16, :] for a in CORNERS], axis=0))
            elif part == "vert":
                cols.append(jnp.concatenate([ref[i, a : a + n, :] for a, n in VERT], axis=0))
            else:
                cols.append(ref[i])
        return jnp.concatenate(cols, axis=1)

    def project(ref, cb, part):
        w = W[pl.ds(cb * KEEP, KEEP)].reshape(KEEP * HD, HD)
        return jnp.dot(rows_of(ref, cb, part), w, preferred_element_type=jnp.float32).astype(jnp.bfloat16)

    def chunk(lo, count, part):
        if part in ("own", "all"):
            @pl.when(lo < HEADS)
            def _():
                for e in range(count):
                    Q[lo + e] = project(NO, lo + e, "q")

        @pl.when(lo >= HEADS)
        def _():
            for e in range(count):
                at = lo + e - HEADS
                r = project(NO if part == "own" else N, lo + e, part)
                if part == "own":
                    for g in range(4):
                        KV[at, 64 * g + 80 : 64 * g + 112, :] = r[32 * g : 32 * g + 32]
                    KV[at, 16:48, :] = r[128:160]
                    KV[at, 336:368, :] = r[160:192]
                elif part == "vert":
                    k = 0
                    for a, n in VERT:
                        KV[at, a : a + n, :] = r[k : k + n]
                        k += n
                elif part == "corners":
                    for k, a in enumerate(CORNERS):
                        KV[at, a : a + 16, :] = r[16 * k : 16 * k + 16]
                else:
                    KV[at] = r

    def shard(f, part):
        def step(c, _):
            chunk(f * SHARD + c * 3, 3, part)
            return 0

        lax.fori_loop(0, SHARD // 3, step, 0)

    def make_shifted():
        SHIFT[0] = jnp.zeros((HEADS, HD), jnp.float32)
        SHIFT[0, :, 0:81] = rel[...]
        v = SHIFT[0]
        lane = lax.broadcasted_iota(jnp.int32, (HEADS, HD), 1)
        rows = [jnp.zeros_like(v)] * 3
        for a in range(9):
            for e in range(3):
                at = (lane + (3 if e == 2 else 0)) % HD
                moved = pltpu.roll(v, (-5 * a - 4 * e) % HD, 1)
                rows[e] = jnp.where((at >= 4 * a) & (at < 4 * a + 4), moved, rows[e])
        SHIFT[0] = rows[0]
        SHIFT[1] = pltpu.roll(rows[0], HD - 4, 1)
        SHIFT[2] = rows[1]
        SHIFT[3] = rows[2]

    def make_bias():
        make_shifted()
        lane = lax.broadcasted_iota(jnp.int32, (8, PAIR), 1)
        sub = lax.broadcasted_iota(jnp.int32, (8, PAIR), 0)
        ky, kx = (lane % 64) // 4 - 4, (lane // 64) * 4 + lane % 4 - 4
        inside = (ky + row * TH >= 0) & (ky + row * TH < 8 * TH)
        low = lax.broadcasted_iota(jnp.int32, (8, HD), 1) < 64
        right = lax.broadcasted_iota(jnp.int32, (8, HD), 1) % 4 >= lax.broadcasted_iota(jnp.int32, (8, HD), 0) % 4
        for i in range(4):
            qy, qx = 2 * i + sub // 4, sub % 4
            ok = inside & (jnp.abs(ky - qy) <= RADIUS) & (jnp.abs(kx - qx) <= RADIUS)

            def step(h, _):
                r = [
                    pltpu.roll(jnp.broadcast_to(SHIFT[e, pl.ds(h, 1), :], (8, HD)), 8 * i, 1, stride=1, stride_axis=0) for e in range(4)
                ]
                same = jnp.where(right, r[2], r[1])
                first = jnp.where(ok[:, :HD], jnp.where(low, r[0], pltpu.roll(same, 64, 1)), NEG)
                last = jnp.where(ok[:, HD:], r[3], NEG)
                turned = pltpu.roll(first, 64, 1)
                B[h, 8 * i : 8 * i + 8, :] = jnp.concatenate([first, jnp.where(low, last, NEG)], axis=1)
                B[h, 32 + 8 * i : 40 + 8 * i, :] = jnp.concatenate([jnp.where(low, NEG, turned), jnp.where(low, turned, pltpu.roll(last, 64, 1))], axis=1)
                return 0

            lax.fori_loop(0, HEADS, step, 0, unroll=4)
        wide = lax.broadcasted_iota(jnp.int32, (8, PAIR), 1)
        EDGE[0] = jnp.where((wide < 64) & (col == 0), NEG, 0.0)
        EDGE[1] = jnp.where((wide >= 192) & (col == 7), NEG, 0.0)

    def attend(h0, count):
        pairs = [(h0 + i, p) for i in range(count) for p in range(2)]
        ss_, ws_, os_ = [], [], []
        for h, p in pairs:
            ss_.append(lax.dot_general(
                Q[h, 64 * p : 64 * p + 64, :], KV[h, 128 * p : 128 * p + PAIR, :], (((1,), (1,)), ((), ())), preferred_element_type=jnp.float32
            ))
        for (h, p), s in zip(pairs, ss_):
            s = s * (HD ** -0.5) + B[h] + EDGE[p, 0:1, :]
            w = jnp.exp(s - jnp.max(s, axis=1, keepdims=True))
            ws_.append((w.astype(jnp.bfloat16), jnp.sum(w, axis=1, keepdims=True)))
        for (h, p), (w, total) in zip(pairs, ws_):
            o = jnp.dot(w, KV[HEADS + h, 128 * p : 128 * p + PAIR, :], preferred_element_type=jnp.float32) / total
            os_.append((o[0:32], o[32:64]))
        for i in range(count):
            outs = os_[2 * i] + os_[2 * i + 1]
            for j in range(4):
                halves = []
                for half in range(2):
                    halves.append(swap_fours(outs[2 * half][8 * j : 8 * j + 8], outs[2 * half + 1][8 * j : 8 * j + 8]))
                for e in range(2):
                    both = jnp.concatenate([halves[0][e], halves[1][e]], axis=0)
                    ATT[h0 + i, 32 * j + 16 * e : 32 * j + 16 * e + 16, :] = both.astype(jnp.bfloat16)

    def output(cb):
        lhs = jnp.concatenate([ATT[OI[j, cb]] for j in range(KEEP_O)], axis=1)
        w = WO[pl.ds(cb * KEEP_O, KEEP_O)].reshape(KEEP_O * HD, HD)
        acc = jnp.dot(lhs, w, preferred_element_type=jnp.float32)
        lanes = pl.ds(pl.multiple_of(cb * HD, HD), HD)
        out[:, lanes] = (acc + NAT[:, lanes].astype(jnp.float32)).astype(jnp.bfloat16)

    c_tok.wait()
    regroup()
    h_start("NR", "SR", "N", "S", "ND", "SD", "W", "E")
    for c in a_starts[4:]:
        c.start()

    @pl.when(jnp.logical_not(up))
    def _():
        T[0:3, 0:16, :] = jnp.zeros((3, 16, 6144), jnp.bfloat16)
        T[5, 0:16, :] = jnp.zeros((16, 6144), jnp.bfloat16)

    @pl.when(jnp.logical_not(down))
    def _():
        T[0:3, 48:64, :] = jnp.zeros((3, 16, 6144), jnp.bfloat16)
        T[5, 48:64, :] = jnp.zeros((16, 6144), jnp.bfloat16)

    @pl.when(jnp.logical_not(west))
    def _():
        T[0] = jnp.zeros((64, 6144), jnp.bfloat16)

    @pl.when(jnp.logical_not(east))
    def _():
        T[5] = jnp.zeros((64, 6144), jnp.bfloat16)

    def pump_x(i):
        for j in (i, 4 + i):
            a_recv(j).wait_recv()
            a_forward(j).start()
            s_send(j).start()

    def pump(*items):
        for j in items:
            a_recv(j).wait_recv()
            s_send(j).start()

    norm_own()
    pump_x(0)
    make_bias()
    pump_x(1)
    h_wait("NR", "SR")
    h_start("NF", "SF")
    h_wait("W", "E")
    norm_edges()
    c_wq.wait()
    c_qi.wait()
    shard(f_own, "own")
    pump_x(2)
    o_starts = [o_first(0), o_first(1)]
    for c in o_starts:
        c.start()
    sb_send.start()
    sa_recv.wait_recv()
    shard(f_sib, "own")
    pump_x(3)
    def base(f, j):
        return f * SHARD + (16 if j == 8 else came[j])

    def received(j, part):
        chunk(base(f_oth, j), 2, part)
        for i in range(2):
            s_recv(j + i).wait_recv()
        chunk(base(f_osb, j), 2, part)

    for j in (0, 4, 2, 6):
        received(j, "own")
    h_wait("N", "S", "ND", "SD", "NF", "SF")
    h_start("NW", "NE", "SW", "SE")
    norm_vertical()
    a_recv(8).wait_recv()
    a_forward(8).start()
    s_send(8).start()
    pump(10, 14)
    shard(f_own, "vert")
    pump(11, 15, 12, 16)
    shard(f_sib, "vert")
    pump(13, 17, 9)
    for j in range(2):
        o_recv(j).wait_recv()
        o_forward(j).start()
        os_send(j).start()

    for j in (0, 4, 2, 6):
        chunk(base(f_oth, j), 2, "vert")
        chunk(base(f_osb, j), 2, "vert")
    h_wait("NW", "NE", "SW", "SE")
    norm_corners()
    shard(f_own, "corners")
    shard(f_sib, "corners")
    for j in (0, 4, 2, 6):
        chunk(base(f_oth, j), 2, "corners")
        chunk(base(f_osb, j), 2, "corners")
    for j in (8, 10, 14, 12, 16):
        received(j, "all")

    def head(i, _):
        attend(3 * i, 3)
        return 0

    lax.fori_loop(0, HEADS // 6, head, 0)
    for j in range(2, 4):
        o_recv(j).wait_recv()
        os_send(j).start()
    lax.fori_loop(HEADS // 6, HEADS // 3, head, 0)
    c_wo.wait()
    c_oi.wait()
    sb_recv.wait_recv()
    for j in range(4):
        os_recv(j).wait_recv()

    def column(cb, _):
        output(cb)
        return 0

    lax.fori_loop(0, GROUPS, column, 0, unroll=4)

    for c in a_starts + o_starts + [sa_send, sb_send]:
        c.wait_send()
    for j in range(9):
        a_forward(j).wait_send()
    for j in range(2):
        o_forward(j).wait_send()
    for j in range(18):
        s_send(j).wait_send()
    for j in range(4):
        os_send(j).wait_send()
    h_wait_send(*names)


def body(tokens, ln_gain, qkv_blocks, qkv_index, out_blocks, out_index, rel_bias):
    any_, vmem = pl.BlockSpec(memory_space=pl.ANY), pl.BlockSpec(memory_space=pltpu.VMEM)
    dma = lambda n: pltpu.SemaphoreType.DMA((n,))
    bf = jnp.bfloat16
    mixed = pl.pallas_call(
        kernel,
        out_shape=jax.ShapeDtypeStruct((OWN, 6144), bf),
        in_specs=[any_, any_, any_, vmem, vmem, any_, any_],
        out_specs=vmem,
        scratch_shapes=[
            pltpu.VMEM((OWN, 6144), bf),
            pltpu.VMEM((6, 64, 6144), bf),
            pltpu.VMEM((GROUPS, ALL, HD), bf),
            pltpu.VMEM((GROUPS, OWN + 64, HD), bf),
            pltpu.VMEM((432, HD, HD), bf),
            pltpu.VMEM((144, HD, HD), bf),
            pltpu.VMEM((HEADS, OWN, HD), bf),
            pltpu.VMEM((2 * HEADS, ALL, HD), bf),
            pltpu.VMEM((HEADS, OWN, HD), bf),
            pltpu.VMEM((HEADS, 64, PAIR), jnp.float32),
            pltpu.VMEM((2, 8, PAIR), jnp.float32),
            pltpu.VMEM((4, HEADS, HD), jnp.float32),
            pltpu.SMEM((KEEP, 3 * HEADS), jnp.int32),
            pltpu.SMEM((KEEP_O, GROUPS), jnp.int32),
            dma(5), dma(14), dma(14), dma(18), dma(18), dma(18), dma(18), dma(4), dma(4), dma(4), dma(4), dma(2), dma(2),
        ],
        compiler_params=pltpu.CompilerParams(collective_id=0, has_side_effects=True, vmem_limit_bytes=58 * 2**20),
        cost_estimate=pl.CostEstimate(flops=6 * 10**9, bytes_accessed=30 * 2**20, transcendentals=10**6),
        name="block",
    )(
        qkv_index.T, out_index.T, tokens.reshape(OWN, -1), ln_gain.reshape(1, -1), rel_bias,
        qkv_blocks.reshape(SHARD * KEEP, HD, HD), out_blocks.reshape(SHARD_O * KEEP_O, HD, HD),
    )
    return mixed.reshape(1, TH, TW, -1)


def solution(mesh):
    in_specs = (
        P("fsdp", "row", "col", None),
        P(),
        P("fsdp", None, None, None),
        P(),
        P("fsdp", None, None, None),
        P(),
        P(),
    )
    out_specs = P("fsdp", "row", "col", None)
    return jax.shard_map(body, mesh=mesh, in_specs=in_specs, out_specs=out_specs, check_vma=False)
```
